32 devices in a mesh: row: 8 (over z, core), col: 4 (over y, x).
Axes of the slice: x: 2, y: 2, z: 4, core: 2. Of those that a mesh axis runs over, the one named last changes fastest.
Arguments:
- tokens: bfloat16 [256, 8192], P('col', 'row'), may hold values from -6 to 6
- gate_weight: bfloat16 [8192, 26624], P('row', 'col'), may hold values from -0.0625 to 0.0625
- up_weight: bfloat16 [8192, 26624], P('row', 'col'), may hold values from -0.0625 to 0.0625
- down_weight: bfloat16 [26624, 8192], P('col', 'row'), may hold values from -0.0390625 to 0.0390625
- cotangent: bfloat16 [256, 8192], P('col', 'row'), may hold values from -3 to 3
Outputs:
- mixed: bfloat16 [256, 8192], P('col', 'row')
- grad_tokens: bfloat16 [256, 8192], P('col', 'row')
- grad_gate: bfloat16 [8192, 26624], P('row', 'col')
- grad_up: bfloat16 [8192, 26624], P('row', 'col')
- grad_down: bfloat16 [26624, 8192], P('col', 'row')
The draws below stay inside these ranges and needn't reach their ends.
All inputs are finite; a program needn't handle non-finite values.
Results may differ from the reference program's by a relative error of at most 0.019.
Values may be sent and summed in bfloat16 or wider, within the bound.
No kernel may reach another device: no remote copies, remote signals or barrier semaphores. Data moves between devices by JAX's collectives and lax.ppermute only.
A program may use at most 192 MiB of HBM per device.

```python
import jax
import jax.numpy as jnp

D = 8192
FF = 26624
TOKENS = 256


def levels(rng, dims, split, low, high):
    factor_of = 1.0
    for position, parts in split:
        heights = jax.random.uniform(jax.random.fold_in(jax.random.fold_in(rng, 6), position), (parts,), jnp.float32, low / len(split), high / len(split))
        factor_of = factor_of * jnp.repeat(jnp.exp(heights), dims[position] // parts).reshape((-1,) + (1,) * (len(dims) - 1 - position))
    return factor_of


def scatter_about(key, dims, scale, reach, cuts=(), dtype=jnp.bfloat16):
    drawn = scale * jax.random.normal(key, dims, jnp.float32)
    if cuts:
        drawn = drawn * levels(key, dims, cuts, -0.22, 0.18)
    return jnp.clip(drawn, -reach, reach).astype(dtype)


def setup_inputs(seed: int = 0) -> dict:
    key_of = jax.random.split(jax.random.key(seed), 6)
    tokens = scatter_about(key_of[0], (TOKENS, D), 1.0, 6.0, ((0, 4), (1, 8)))
    gate_weight = scatter_about(key_of[1], (D, FF), D ** -0.5, 0.0625, ((0, 8), (1, 4)))
    up_weight = scatter_about(key_of[2], (D, FF), D ** -0.5, 0.0625, ((0, 8), (1, 4)))
    down_weight = scatter_about(key_of[3], (FF, D), FF ** -0.5, 0.0390625, ((0, 4), (1, 8)))
    cotangent = scatter_about(key_of[4], (TOKENS, D), 0.5, 3.0, ((0, 4), (1, 8)))
    return dict(tokens=tokens, gate_weight=gate_weight, up_weight=up_weight, down_weight=down_weight, cotangent=cotangent)


def reference(tokens, gate_weight, up_weight, down_weight, cotangent):
    gate_sum = jnp.dot(tokens, gate_weight, preferred_element_type=jnp.float32)
    up_sum = jnp.dot(tokens, up_weight, preferred_element_type=jnp.float32)
    back_sum = jnp.dot(cotangent, down_weight.T, preferred_element_type=jnp.float32)
    sigma = jax.nn.sigmoid(gate_sum)
    hidden = (gate_sum * sigma * up_sum).astype(jnp.bfloat16)
    mixed = jnp.dot(hidden, down_weight, preferred_element_type=jnp.float32).astype(jnp.bfloat16)
    grad_up_act = (back_sum * gate_sum * sigma).astype(jnp.bfloat16)
    grad_gate_act = (back_sum * up_sum * sigma * (1.0 + gate_sum * (1.0 - sigma))).astype(jnp.bfloat16)
    grad_tokens = (jnp.dot(grad_gate_act, gate_weight.T, preferred_element_type=jnp.float32)
                   + jnp.dot(grad_up_act, up_weight.T, preferred_element_type=jnp.float32)).astype(jnp.bfloat16)
    grad_gate = jnp.dot(tokens.T, grad_gate_act, preferred_element_type=jnp.float32).astype(jnp.bfloat16)
    grad_up = jnp.dot(tokens.T, grad_up_act, preferred_element_type=jnp.float32).astype(jnp.bfloat16)
    grad_down = jnp.dot(hidden.T, cotangent, preferred_element_type=jnp.float32).astype(jnp.bfloat16)
    return mixed, grad_tokens, grad_gate, grad_up, grad_down
```

```python
import functools

import jax
import jax.numpy as jnp
from jax import lax
from jax.experimental import pallas as pl
from jax.experimental.pallas import tpu as pltpu
from jax.sharding import PartitionSpec as P

F32 = jnp.float32
BF16 = jnp.bfloat16
LANES = 128
CHUNKS = 13
VMEM_LIMIT = 40 * 1024 * 1024


def tile_of(width):
    return 256 if width % 256 == 0 else LANES


def contract_last(left, right):
    return lax.dot_general(left, right, (((1,), (1,)), ((), ())), preferred_element_type=F32)


def contract_first(left, right):
    return lax.dot_general(left, right, (((0,), (0,)), ((), ())), preferred_element_type=F32)


def whole(shape):
    return pl.BlockSpec(shape, lambda i: (0,) * len(shape))


def forward_kernel(x_ref, c_ref, gate_ref, up_ref, down_ref, mine_ref, theirs_ref):
    half = mine_ref.shape[1]
    sums = (
        jnp.dot(x_ref[...], gate_ref[...], preferred_element_type=F32),
        jnp.dot(x_ref[...], up_ref[...], preferred_element_type=F32),
        contract_last(c_ref[...], down_ref[...]),
    )
    for index, value in enumerate(sums):
        mine_ref[index] = value[:half].astype(BF16)
        theirs_ref[index] = value[half:].astype(BF16)


def forward(x, c, gate, up, down, start, width):
    tokens, depth = x.shape
    tile = tile_of(width)
    first = start // tile
    half = tokens // 2
    part = jax.ShapeDtypeStruct((3, half, width), BF16)
    column = pl.BlockSpec((depth, tile), lambda i: (0, first + i))
    piece = pl.BlockSpec((3, half, tile), lambda i: (0, 0, i))
    return pl.pallas_call(
        forward_kernel,
        grid=(width // tile,),
        in_specs=[
            whole(x.shape),
            whole(c.shape),
            column,
            column,
            pl.BlockSpec((tile, depth), lambda i: (first + i, 0)),
        ],
        out_specs=[piece, piece],
        out_shape=[part, part],
        compiler_params=pltpu.CompilerParams(vmem_limit_bytes=VMEM_LIMIT),
        cost_estimate=pl.CostEstimate(
            flops=6 * tokens * depth * width,
            bytes_accessed=6 * depth * width + 4 * tokens * depth + 6 * tokens * width,
            transcendentals=0,
        ),
        name="forward_sums",
    )(x, c, gate, up, down)


def activation_kernel(left_ref, right_ref, out_ref):
    gate_sum, up_sum, back_sum = (
        left_ref[i].astype(F32) + right_ref[i].astype(F32) for i in range(3)
    )
    sigma = jax.nn.sigmoid(gate_sum)
    silu = gate_sum * sigma
    out_ref[0] = (silu * up_sum).astype(BF16)
    out_ref[1] = (back_sum * up_sum * sigma * (1.0 + gate_sum * (1.0 - sigma))).astype(BF16)
    out_ref[2] = (back_sum * silu).astype(BF16)


def activations(left, right):
    _, half, width = left.shape
    tile = tile_of(width)
    piece = pl.BlockSpec((3, half, tile), lambda i: (0, 0, i))
    return pl.pallas_call(
        activation_kernel,
        grid=(width // tile,),
        in_specs=[piece, piece],
        out_specs=piece,
        out_shape=jax.ShapeDtypeStruct(left.shape, BF16),
        compiler_params=pltpu.CompilerParams(vmem_limit_bytes=VMEM_LIMIT),
        cost_estimate=pl.CostEstimate(
            flops=12 * half * width, bytes_accessed=18 * half * width, transcendentals=half * width
        ),
        name="activations",
    )(left, right)


def backward_kernel(n_fixed, *refs):
    (mine_ref, other_ref, xt_ref, c_ref, gate_ref, up_ref, down_ref) = refs[:7]
    total_ref, grad_gate_ref, grad_up_ref, grad_down_ref = refs[-4:]

    @pl.when(pl.program_id(0) == 0)
    def _():
        if n_fixed:
            total_ref[...] = refs[7][...]
        else:
            total_ref[...] = jnp.zeros_like(total_ref)

    hidden, gate_act, up_act = (
        jnp.concatenate([mine_ref[i], other_ref[i]], axis=0) for i in range(3)
    )
    total_ref[0] += jnp.dot(hidden, down_ref[...], preferred_element_type=F32)
    total_ref[1] += contract_last(gate_act, gate_ref[...]) + contract_last(up_act, up_ref[...])
    grad_gate_ref[...] = jnp.dot(xt_ref[...], gate_act, preferred_element_type=F32).astype(BF16)
    grad_up_ref[...] = jnp.dot(xt_ref[...], up_act, preferred_element_type=F32).astype(BF16)
    grad_down_ref[...] = contract_first(hidden, c_ref[...]).astype(BF16)


def backward(mine, other, xt, c, gate, up, down, start, previous):
    tokens, depth = c.shape
    _, half, width = mine.shape
    tile = tile_of(width)
    first = start // tile
    piece = pl.BlockSpec((3, half, tile), lambda i: (0, 0, i))
    column = pl.BlockSpec((depth, tile), lambda i: (0, first + i))
    row = pl.BlockSpec((tile, depth), lambda i: (first + i, 0))
    total_spec = whole((2, tokens, depth))
    anywhere = pl.BlockSpec(memory_space=pl.ANY)
    extra_specs = [total_spec, anywhere, anywhere, anywhere] if previous else []
    return pl.pallas_call(
        functools.partial(backward_kernel, len(previous)),
        grid=(width // tile,),
        in_specs=[piece, piece, whole(xt.shape), whole(c.shape), column, column, row] + extra_specs,
        out_specs=[total_spec, column, column, row],
        out_shape=[
            jax.ShapeDtypeStruct((2, tokens, depth), F32),
            jax.ShapeDtypeStruct(gate.shape, BF16),
            jax.ShapeDtypeStruct(up.shape, BF16),
            jax.ShapeDtypeStruct(down.shape, BF16),
        ],
        input_output_aliases={7 + i: i for i in range(len(previous))},
        compiler_params=pltpu.CompilerParams(vmem_limit_bytes=VMEM_LIMIT),
        cost_estimate=pl.CostEstimate(
            flops=12 * tokens * depth * width,
            bytes_accessed=12 * depth * width + 20 * tokens * depth + 6 * tokens * width,
            transcendentals=0,
        ),
        name="backward_products",
    )(mine, other, xt, c, gate, up, down, *previous)


def add(left, right):
    return (left.astype(F32) + right.astype(F32)).astype(BF16)


def both_ways(chips, pairs):
    return [(2 * a + core, 2 * b + core) for a, b in pairs for core in range(2)]


def shards(n_row, n_col, tokens, gate_weight, up_weight, down_weight, cotangent):
    chips = n_row // 2
    middle = chips // 2
    core = lax.axis_index("row") % 2
    chip = lax.axis_index("row") // 2
    siblings = [(r, r ^ 1) for r in range(n_row)]
    inward = [
        both_ways(chips, [(j, j + 1), (chips - 1 - j, chips - 2 - j)]) for j in range(middle - 1)
    ]
    across = both_ways(chips, [(middle - 1, middle), (middle, middle - 1)])

    def gather(block):
        blocks = [block] + [
            lax.ppermute(block, "col", [(s, s ^ j) for s in range(n_col)]) for j in range(1, n_col)
        ]
        low = jnp.concatenate(blocks[: n_col // 2], axis=0)
        high = jnp.concatenate(blocks[n_col // 2 :], axis=0)
        return jnp.concatenate(
            [jnp.where(core == 0, low, high), jnp.where(core == 0, high, low)], axis=0
        )

    x = gather(tokens)
    c = gather(cotangent)
    xt = x.T

    hidden_units = gate_weight.shape[1]
    width = hidden_units // CHUNKS
    result = []
    for k in range(CHUNKS):
        start = k * width
        mine, theirs = forward(x, c, gate_weight, up_weight, down_weight, start, width)
        partial = add(mine, lax.ppermute(theirs, "row", siblings))
        for hop in inward:
            partial = add(partial, lax.ppermute(partial, "row", hop))
        act = activations(partial, lax.ppermute(partial, "row", across))
        for j in reversed(range(middle - 1)):
            arrived = lax.ppermute(act, "row", [(t, s) for s, t in inward[j]])
            act = jnp.where((chip == j) | (chip == chips - 1 - j), arrived, act)
        other = lax.ppermute(act, "row", siblings)
        result = backward(act, other, xt, c, gate_weight, up_weight, down_weight, start, result)

    total, grad_gate, grad_up, grad_down = result
    half = total.shape[1] // 2
    block = total.shape[1] // n_col
    total = total.astype(BF16)
    ordered = jnp.where(
        core == 0, total, jnp.concatenate([total[:, half:], total[:, :half]], axis=1)
    )
    out = ordered[:, :block].astype(F32)
    for j in range(1, n_col):
        piece = ordered[:, j * block : (j + 1) * block]
        out += lax.ppermute(piece, "col", [(s, s ^ j) for s in range(n_col)]).astype(F32)
    out = out.astype(BF16)
    return out[0], out[1], grad_gate, grad_up, grad_down


def solution(mesh):
    in_specs = (P("col", "row"), P("row", "col"), P("row", "col"), P("col", "row"), P("col", "row"))
    out_specs = (
        P("col", "row"),
        P("col", "row"),
        P("row", "col"),
        P("row", "col"),
        P("col", "row"),
    )
    return jax.shard_map(
        functools.partial(shards, mesh.shape["row"], mesh.shape["col"]),
        mesh=mesh,
        in_specs=in_specs,
        out_specs=out_specs,
        check_vma=False,
    )
```

```python
import functools

import jax
import jax.numpy as jnp
from jax import lax
from jax.experimental import pallas as pl
from jax.experimental.pallas import tpu as pltpu
from jax.sharding import PartitionSpec as P

F32 = jnp.float32
BF16 = jnp.bfloat16
MOST_CHUNKS = 9
PRODUCT_VMEM = 40 * 1024 * 1024
SMALL_VMEM = 10 * 1024 * 1024
ANYWHERE = pl.BlockSpec(memory_space=pl.ANY)


def unit_of(hidden_units):
    return 256 if hidden_units % 256 == 0 else 128


def chunks_of(hidden_units):
    unit = unit_of(hidden_units)
    width = -(-(hidden_units // unit) // MOST_CHUNKS) * unit
    return [(s, min(width, hidden_units - s)) for s in range(0, hidden_units, width)]


def tile_of(width):
    return 256 if width % 256 == 0 else 128


def whole(shape):
    return pl.BlockSpec(shape, lambda i: (0,) * len(shape))


class Order:
    def __init__(self):
        self.last = None

    def call(self, kernel, grid, in_specs, out_specs, out_shape, aliases, vmem, cost, name, *args):
        extra = [] if self.last is None else [self.last]

        def body(*refs):
            kernel(*refs[: len(args)], *refs[len(args) + len(extra) :])

        out = pl.pallas_call(
            body,
            grid=grid,
            in_specs=list(in_specs) + [ANYWHERE] * len(extra),
            out_specs=out_specs,
            out_shape=out_shape,
            input_output_aliases=aliases,
            compiler_params=pltpu.CompilerParams(vmem_limit_bytes=vmem),
            cost_estimate=pl.CostEstimate(flops=cost, bytes_accessed=cost, transcendentals=0),
            name=name,
        )(*args, *extra)
        self.last = out[0]
        return out


def forward_kernel(x_ref, ct_ref, gate_ref, up_ref, down_ref, mine_ref, theirs_ref):
    half = mine_ref.shape[1]
    sums = (
        jnp.dot(x_ref[...], gate_ref[...], preferred_element_type=F32),
        jnp.dot(x_ref[...], up_ref[...], preferred_element_type=F32),
        jnp.dot(down_ref[...], ct_ref[...], preferred_element_type=F32).T,
    )
    for index, value in enumerate(sums):
        mine_ref[index] = value[:half].astype(BF16)
        theirs_ref[index] = value[half:].astype(BF16)


def forward(order, x, ct, gate, up, down, start, width):
    tokens, depth = x.shape
    tile = tile_of(width)
    first = start // tile
    half = tokens // 2
    part = jax.ShapeDtypeStruct((3, half, width), BF16)
    column = pl.BlockSpec((depth, tile), lambda i: (0, first + i))
    row = pl.BlockSpec((tile, depth), lambda i: (first + i, 0))
    piece = pl.BlockSpec((3, half, tile), lambda i: (0, 0, i))
    return order.call(
        forward_kernel,
        (width // tile,),
        [whole(x.shape), whole(ct.shape), column, column, row],
        [piece, piece],
        [part, part],
        {},
        PRODUCT_VMEM,
        1000,
        "forward_sums",
        x, ct, gate, up, down,
    )


def elementwise(order, kernel, name, *args):
    _, half, width = args[0].shape
    tile = tile_of(width)
    piece = pl.BlockSpec((3, half, tile), lambda i: (0, 0, i))
    specs = [piece if a.ndim == 3 else pl.BlockSpec(memory_space=pltpu.SMEM) for a in args]
    shape = jax.ShapeDtypeStruct(args[0].shape, BF16)
    return order.call(
        kernel, (width // tile,), specs, [piece], [shape], {}, SMALL_VMEM, 1000, name, *args
    )[0]


def add_kernel(left_ref, right_ref, out_ref):
    out_ref[...] = (left_ref[...].astype(F32) + right_ref[...].astype(F32)).astype(BF16)


def choose_kernel(left_ref, flag_ref, right_ref, out_ref):
    @pl.when(flag_ref[0] == 0)
    def _():
        out_ref[...] = left_ref[...]

    @pl.when(flag_ref[0] != 0)
    def _():
        out_ref[...] = right_ref[...]


def activation_kernel(left_ref, right_ref, out_ref):
    gate_sum, up_sum, back_sum = (
        left_ref[i].astype(F32) + right_ref[i].astype(F32) for i in range(3)
    )
    sigma = jax.nn.sigmoid(gate_sum)
    silu = gate_sum * sigma
    out_ref[0] = (silu * up_sum).astype(BF16)
    out_ref[1] = (back_sum * up_sum * sigma * (1.0 + gate_sum * (1.0 - sigma))).astype(BF16)
    out_ref[2] = (back_sum * silu).astype(BF16)


def joined(mine_ref, other_ref):
    return [jnp.concatenate([mine_ref[i], other_ref[i]], axis=0) for i in range(3)]


def token_products(acts, weight_refs, before_refs, mixed_ref, inputs_ref):
    gate_ref, up_ref, down_ref = weight_refs

    @pl.when(pl.program_id(0) == 0)
    def _():
        if not before_refs:
            mixed_ref[...] = jnp.zeros_like(mixed_ref)
            inputs_ref[...] = jnp.zeros_like(inputs_ref)

    hidden, gate_act, up_act = acts
    mixed_ref[...] += jnp.dot(hidden, down_ref[...], preferred_element_type=F32)
    inputs_ref[...] += jnp.dot(
        gate_ref[...], gate_act.T, preferred_element_type=F32
    ) + jnp.dot(up_ref[...], up_act.T, preferred_element_type=F32)


def weight_products(acts, xt_ref, c_ref, grad_gate_ref, grad_up_ref, grad_down_ref):
    hidden, gate_act, up_act = acts
    grad_gate_ref[...] = jnp.dot(xt_ref[...], gate_act, preferred_element_type=F32).astype(BF16)
    grad_up_ref[...] = jnp.dot(xt_ref[...], up_act, preferred_element_type=F32).astype(BF16)
    grad_down_ref[...] = jnp.dot(hidden.T, c_ref[...], preferred_element_type=F32).astype(BF16)


def backward(order, mine, other, xt, c, weights, start, totals, grads, parts):
    _, half, width = mine.shape
    tile = tile_of(width)
    first = start // tile
    piece = pl.BlockSpec((3, half, tile), lambda i: (0, 0, i))
    column = pl.BlockSpec((c.shape[1], tile), lambda i: (0, first + i))
    row = pl.BlockSpec((tile, c.shape[1]), lambda i: (first + i, 0))
    resident = pl.BlockSpec(memory_space=pltpu.VMEM)
    with_tokens, with_weights = "tokens" in parts, "weights" in parts
    specs, args, out_specs, shapes, aliases = [piece, piece], [mine, other], [], [], {}
    if with_tokens:
        specs += [column, column, row]
        args += weights
        for index, total in enumerate(totals or ()):
            aliases[len(args)] = index
            specs += [resident]
            args += [total]
        out_specs += [resident, resident]
        shapes += [jax.ShapeDtypeStruct(a.shape, F32) for a in (c, xt)]
    n_token_args = len(args)
    if with_weights:
        specs += [whole(xt.shape), whole(c.shape)]
        args += [xt, c]
        for index, grad in enumerate(grads or ()):
            aliases[len(args)] = len(out_specs) + index
            specs += [ANYWHERE]
            args += [grad]
        out_specs += [column, column, row]
        shapes += [jax.ShapeDtypeStruct(w.shape, BF16) for w in weights]

    def kernel(*refs):
        ins, outs = refs[: len(args)], refs[len(args) :]
        acts = joined(*ins[:2])
        if with_tokens:
            token_products(acts, ins[2:5], ins[5:n_token_args], *outs[:2])
        if with_weights:
            weight_products(acts, *ins[n_token_args : n_token_args + 2], *outs[-3:])

    out = order.call(
        kernel, (width // tile,), specs, out_specs, shapes, aliases, PRODUCT_VMEM, 1000,
        "backward_products", *args,
    )
    return (out[:2] if with_tokens else totals), (out[-3:] if with_weights else grads)


def both_cores(pairs):
    return [(2 * a + core, 2 * b + core) for a, b in pairs for core in range(2)]


def shards(n_row, n_col, tokens, gate_weight, up_weight, down_weight, cotangent):
    chips = n_row // 2
    middle = chips // 2
    core = lax.axis_index("row") % 2
    chip = lax.axis_index("row") // 2
    siblings = [(r, r ^ 1) for r in range(n_row)]
    inward = [both_cores([(j, j + 1), (chips - 1 - j, chips - 2 - j)]) for j in range(middle - 1)]
    across = both_cores([(middle - 1, middle), (middle, middle - 1)])
    flags = [
        jnp.where((chip == j) | (chip == chips - 1 - j), 1, 0).astype(jnp.int32).reshape(1)
        for j in range(middle - 1)
    ]
    weights = [gate_weight, up_weight, down_weight]

    def gather(block):
        blocks = [block] + [
            lax.ppermute(block, "col", [(s, s ^ j) for s in range(n_col)]) for j in range(1, n_col)
        ]
        low = jnp.concatenate(blocks[: n_col // 2], axis=0)
        high = jnp.concatenate(blocks[n_col // 2 :], axis=0)
        return jnp.concatenate(
            [jnp.where(core == 0, low, high), jnp.where(core == 0, high, low)], axis=0
        )

    x = gather(tokens)
    c = gather(cotangent)
    xt, ct = x.T, c.T

    order = Order()
    chunks = chunks_of(gate_weight.shape[1])
    count = len(chunks)
    swapped, partial, arrived, acts, other = {}, {}, {}, {}, {}
    state = [None, None]

    def step_sums(k):
        if 0 <= k < count:
            mine, theirs = forward(order, x, ct, *weights, *chunks[k])
            swapped[k] = (mine, lax.ppermute(theirs, "row", siblings))

    def step_chip(k):
        if 0 <= k < count:
            partial[k] = elementwise(order, add_kernel, "chip_sum", *swapped.pop(k))
            if inward:
                arrived[k] = lax.ppermute(partial[k], "row", inward[0])

    def step_half(k):
        if 0 <= k < count:
            for hop in range(len(inward)):
                partial[k] = elementwise(order, add_kernel, "half_sum", partial[k], arrived[k])
                if hop + 1 < len(inward):
                    arrived[k] = lax.ppermute(partial[k], "row", inward[hop + 1])
            arrived[k] = lax.ppermute(partial[k], "row", across)

    def step_act(k):
        if 0 <= k < count:
            acts[k] = elementwise(
                order, activation_kernel, "activations", partial.pop(k), arrived.pop(k)
            )
            if inward:
                back = [(t, s) for s, t in inward[-1]]
                arrived[k] = lax.ppermute(acts[k], "row", back)

    def step_choose(k):
        if 0 <= k < count:
            for hop in reversed(range(len(inward))):
                acts[k] = elementwise(
                    order, choose_kernel, "choose", acts[k], flags[hop], arrived[k]
                )
                if hop > 0:
                    back = [(t, s) for s, t in inward[hop - 1]]
                    arrived[k] = lax.ppermute(acts[k], "row", back)
            other[k] = lax.ppermute(acts[k], "row", siblings)

    def step_back(k, parts=("tokens", "weights")):
        if 0 <= k < count:
            state[0], state[1] = backward(
                order, acts[k], other[k], xt, c, weights, chunks[k][0], *state, parts
            )

    step_sums(0)
    step_sums(1)
    step_chip(0)
    step_sums(2)
    step_chip(1)
    step_sums(3)
    for k in range(count + 2):
        step_half(k)
        step_act(k - 1)
        step_chip(k + 2)
        step_sums(k + 4)
        if k - 3 < count - 1:
            step_back(k - 3)
        step_choose(k - 2)
    step_back(count - 1, ("tokens",))
    mixed, inputs = state[0]
    total = jnp.stack([mixed, inputs.T])

    half = total.shape[1] // 2
    block = total.shape[1] // n_col
    total = total.astype(BF16)
    ordered = jnp.where(
        core == 0, total, jnp.concatenate([total[:, half:], total[:, :half]], axis=1)
    )
    out = ordered[:, :block].astype(F32)
    for j in range(1, n_col):
        piece = ordered[:, j * block : (j + 1) * block]
        out += lax.ppermute(piece, "col", [(s, s ^ j) for s in range(n_col)]).astype(F32)
    out = out.astype(BF16)
    step_back(count - 1, ("weights",))
    return out[0], out[1], *state[1]


def solution(mesh):
    in_specs = (P("col", "row"), P("row", "col"), P("row", "col"), P("col", "row"), P("col", "row"))
    out_specs = (
        P("col", "row"),
        P("col", "row"),
        P("row", "col"),
        P("row", "col"),
        P("col", "row"),
    )
    return jax.shard_map(
        functools.partial(shards, mesh.shape["row"], mesh.shape["col"]),
        mesh=mesh,
        in_specs=in_specs,
        out_specs=out_specs,
        check_vma=False,
    )
```

```python
import functools

import jax
import jax.numpy as jnp
from jax import lax
from jax.experimental import pallas as pl
from jax.experimental.pallas import tpu as pltpu
from jax.sharding import PartitionSpec as P

F32 = jnp.float32
BF16 = jnp.bfloat16
MOST_CHUNKS = 9
KERNEL_VMEM = 42 * 1024 * 1024
ANYWHERE = pl.BlockSpec(memory_space=pl.ANY)


def unit_of(hidden_units):
    return 256 if hidden_units % 256 == 0 else 128


def chunks_of(hidden_units):
    unit = unit_of(hidden_units)
    width = -(-(hidden_units // unit) // MOST_CHUNKS) * unit
    return [(s, min(width, hidden_units - s)) for s in range(0, hidden_units, width)]


def tile_of(width):
    return 256 if width % 256 == 0 else 128


def contract_last(left, right):
    return lax.dot_general(left, right, (((1,), (1,)), ((), ())), preferred_element_type=F32)


def whole(shape):
    return pl.BlockSpec(shape, lambda i: (0,) * len(shape))


class Order:
    def __init__(self):
        self.last = None

    def call(self, kernel, grid, in_specs, out_specs, out_shape, aliases, vmem, cost, name, *args):
        extra = [] if self.last is None or any(self.last is a for a in args) else [self.last]

        def body(*refs):
            kernel(*refs[: len(args)], *refs[len(args) + len(extra) :])

        out = pl.pallas_call(
            body,
            grid=grid,
            in_specs=list(in_specs) + [ANYWHERE] * len(extra),
            out_specs=out_specs,
            out_shape=out_shape,
            input_output_aliases=aliases,
            compiler_params=pltpu.CompilerParams(vmem_limit_bytes=vmem),
            cost_estimate=pl.CostEstimate(flops=cost, bytes_accessed=cost, transcendentals=0),
            name=name,
        )(*args, *extra)
        self.last = out[0]
        return out


def forward_kernel(x_ref, c_ref, gate_ref, up_ref, down_ref, mine_ref, theirs_ref):
    half = mine_ref.shape[1]
    sums = (
        jnp.dot(x_ref[...], gate_ref[...], preferred_element_type=F32),
        jnp.dot(x_ref[...], up_ref[...], preferred_element_type=F32),
        contract_last(c_ref[...], down_ref[...]),
    )
    for index, value in enumerate(sums):
        mine_ref[index] = value[:half].astype(BF16)
        theirs_ref[index] = value[half:].astype(BF16)


def forward(order, x, c, gate, up, down, start, width):
    tokens, depth = x.shape
    tile = tile_of(width)
    first = start // tile
    half = tokens // 2
    part = jax.ShapeDtypeStruct((3, half, width), BF16)
    column = pl.BlockSpec((depth, tile), lambda i: (0, first + i))
    row = pl.BlockSpec((tile, depth), lambda i: (first + i, 0))
    piece = pl.BlockSpec((3, half, tile), lambda i: (0, 0, i))
    return order.call(
        forward_kernel,
        (width // tile,),
        [whole(x.shape), whole(c.shape), column, column, row],
        [piece, piece],
        [part, part],
        {},
        KERNEL_VMEM,
        1000,
        "forward_sums",
        x, c, gate, up, down,
    )


def elementwise(order, kernel, name, *args):
    piece = whole(args[0].shape)
    specs = [piece if a.ndim == 3 else pl.BlockSpec(memory_space=pltpu.SMEM) for a in args]
    shape = jax.ShapeDtypeStruct(args[0].shape, BF16)
    return order.call(
        kernel, (1,), specs, [piece], [shape], {}, KERNEL_VMEM, 1000, name, *args
    )[0]


def add_kernel(left_ref, right_ref, out_ref):
    out_ref[...] = (left_ref[...].astype(F32) + right_ref[...].astype(F32)).astype(BF16)


def choose_kernel(left_ref, flag_ref, right_ref, out_ref):
    @pl.when(flag_ref[0] == 0)
    def _():
        out_ref[...] = left_ref[...]

    @pl.when(flag_ref[0] != 0)
    def _():
        out_ref[...] = right_ref[...]


def activation_kernel(left_ref, right_ref, out_ref):
    gate_sum, up_sum, back_sum = (
        left_ref[i].astype(F32) + right_ref[i].astype(F32) for i in range(3)
    )
    sigma = jax.nn.sigmoid(gate_sum)
    silu = gate_sum * sigma
    out_ref[0] = (silu * up_sum).astype(BF16)
    out_ref[1] = (back_sum * up_sum * sigma * (1.0 + gate_sum * (1.0 - sigma))).astype(BF16)
    out_ref[2] = (back_sum * silu).astype(BF16)


def joined(mine_ref, other_ref):
    return [jnp.concatenate([mine_ref[i], other_ref[i]], axis=0) for i in range(3)]


def token_products(acts, weight_refs, before_refs, total_ref):
    gate_ref, up_ref, down_ref = weight_refs
    hidden, gate_act, up_act = acts

    @pl.when(pl.program_id(0) == 0)
    def _():
        if not before_refs:
            total_ref[...] = jnp.zeros_like(total_ref)

    total_ref[0] += jnp.dot(hidden, down_ref[...], preferred_element_type=F32)
    total_ref[1] += contract_last(gate_act, gate_ref[...]) + contract_last(up_act, up_ref[...])


def weight_products(acts, xt_ref, c_ref, grad_gate_ref, grad_up_ref, grad_down_ref):
    hidden, gate_act, up_act = acts
    grad_gate_ref[...] = jnp.dot(xt_ref[...], gate_act, preferred_element_type=F32).astype(BF16)
    grad_up_ref[...] = jnp.dot(xt_ref[...], up_act, preferred_element_type=F32).astype(BF16)
    grad_down_ref[...] = jnp.dot(hidden.T, c_ref[...], preferred_element_type=F32).astype(BF16)


def backward(order, mine, other, xt, c, weights, start, total, grads, parts):
    _, half, width = mine.shape
    tile = tile_of(width)
    first = start // tile
    piece = pl.BlockSpec((3, half, tile), lambda i: (0, 0, i))
    column = pl.BlockSpec((c.shape[1], tile), lambda i: (0, first + i))
    row = pl.BlockSpec((tile, c.shape[1]), lambda i: (first + i, 0))
    resident = pl.BlockSpec(memory_space=pltpu.VMEM)
    with_tokens, with_weights = "tokens" in parts, "weights" in parts
    specs, args, out_specs, shapes, aliases = [piece, piece], [mine, other], [], [], {}
    if with_tokens:
        specs += [column, column, row]
        args += weights
        if total is not None:
            aliases[len(args)] = 0
            specs += [resident]
            args += [total]
        out_specs += [resident]
        shapes += [jax.ShapeDtypeStruct((2,) + c.shape, F32)]
    n_token_args = len(args)
    if with_weights:
        specs += [whole(xt.shape), whole(c.shape)]
        args += [xt, c]
        for index, grad in enumerate(grads or ()):
            aliases[len(args)] = len(out_specs) + index
            specs += [ANYWHERE]
            args += [grad]
        out_specs += [column, column, row]
        shapes += [jax.ShapeDtypeStruct(w.shape, BF16) for w in weights]

    def kernel(*refs):
        ins, outs = refs[: len(args)], refs[len(args) :]
        acts = joined(*ins[:2])
        if with_tokens:
            token_products(acts, ins[2:5], ins[5:n_token_args], outs[0])
        if with_weights:
            weight_products(acts, *ins[n_token_args : n_token_args + 2], *outs[-3:])

    out = order.call(
        kernel, (width // tile,), specs, out_specs, shapes, aliases, KERNEL_VMEM, 1000,
        "backward_products", *args,
    )
    return (out[0] if with_tokens else total), (out[-3:] if with_weights else grads)


def both_cores(pairs):
    return [(2 * a + core, 2 * b + core) for a, b in pairs for core in range(2)]


def shards(n_row, n_col, tokens, gate_weight, up_weight, down_weight, cotangent):
    chips = n_row // 2
    middle = chips // 2
    core = lax.axis_index("row") % 2
    chip = lax.axis_index("row") // 2
    siblings = [(r, r ^ 1) for r in range(n_row)]
    inward = [both_cores([(j, j + 1), (chips - 1 - j, chips - 2 - j)]) for j in range(middle - 1)]
    across = both_cores([(middle - 1, middle), (middle, middle - 1)])
    flags = [
        jnp.where((chip == j) | (chip == chips - 1 - j), 1, 0).astype(jnp.int32).reshape(1)
        for j in range(middle - 1)
    ]
    weights = [gate_weight, up_weight, down_weight]

    def gather(block):
        blocks = [block] + [
            lax.ppermute(block, "col", [(s, s ^ j) for s in range(n_col)]) for j in range(1, n_col)
        ]
        low = jnp.concatenate(blocks[: n_col // 2], axis=0)
        high = jnp.concatenate(blocks[n_col // 2 :], axis=0)
        return jnp.concatenate(
            [jnp.where(core == 0, low, high), jnp.where(core == 0, high, low)], axis=0
        )

    x = gather(tokens)
    c = gather(cotangent)
    xt = x.T

    order = Order()
    chunks = chunks_of(gate_weight.shape[1])
    count = len(chunks)
    swapped, partial, arrived, acts, other = {}, {}, {}, {}, {}
    state = [None, None]

    def step_sums(k):
        if 0 <= k < count:
            mine, theirs = forward(order, x, c, *weights, *chunks[k])
            swapped[k] = (mine, lax.ppermute(theirs, "row", siblings))

    def step_chip(k):
        if 0 <= k < count:
            partial[k] = elementwise(order, add_kernel, "chip_sum", *swapped.pop(k))
            if inward:
                arrived[k] = lax.ppermute(partial[k], "row", inward[0])

    def step_half(k):
        if 0 <= k < count:
            for hop in range(len(inward)):
                partial[k] = elementwise(order, add_kernel, "half_sum", partial[k], arrived[k])
                if hop + 1 < len(inward):
                    arrived[k] = lax.ppermute(partial[k], "row", inward[hop + 1])
            arrived[k] = lax.ppermute(partial[k], "row", across)

    def step_act(k):
        if 0 <= k < count:
            acts[k] = elementwise(
                order, activation_kernel, "activations", partial.pop(k), arrived.pop(k)
            )
            if inward:
                back = [(t, s) for s, t in inward[-1]]
                arrived[k] = lax.ppermute(acts[k], "row", back)

    def step_choose(k):
        if 0 <= k < count:
            for hop in reversed(range(len(inward))):
                acts[k] = elementwise(
                    order, choose_kernel, "choose", acts[k], flags[hop], arrived[k]
                )
                if hop > 0:
                    back = [(t, s) for s, t in inward[hop - 1]]
                    arrived[k] = lax.ppermute(acts[k], "row", back)
            other[k] = lax.ppermute(acts[k], "row", siblings)

    def step_back(k, parts=("tokens", "weights")):
        if 0 <= k < count:
            state[0], state[1] = backward(
                order, acts[k], other[k], xt, c, weights, chunks[k][0], *state, parts
            )

    step_sums(0)
    step_sums(1)
    step_chip(0)
    step_chip(1)
    summed = 2
    deferred = [k for k in range(count - 6, count - 3) if k >= 0] + [count - 1]
    for k in range(count):
        fresh = range(summed, min(count, summed + (3 if k == 0 else 2)))
        summed = fresh.stop
        for j in fresh:
            step_sums(j)
        step_half(k)
        step_act(k - 1)
        step_choose(k - 2)
        for j in fresh:
            step_chip(j)
        step_back(k - 3, ("tokens",) if k - 3 in deferred else ("tokens", "weights"))
    for k in deferred[:2]:
        step_back(k, ("weights",))
    step_act(count - 1)
    step_choose(count - 2)
    step_back(count - 3)
    step_back(count - 2)
    step_choose(count - 1)
    step_back(count - 1, ("tokens",))
    total = state[0]

    half = total.shape[1] // 2
    block = total.shape[1] // n_col
    total = total.astype(BF16)
    ordered = jnp.where(
        core == 0, total, jnp.concatenate([total[:, half:], total[:, :half]], axis=1)
    )
    out = ordered[:, :block].astype(F32)
    for j in range(1, n_col):
        piece = ordered[:, j * block : (j + 1) * block]
        out += lax.ppermute(piece, "col", [(s, s ^ j) for s in range(n_col)]).astype(F32)
    out = out.astype(BF16)
    for k in deferred[2:]:
        step_back(k, ("weights",))
    return out[0], out[1], *state[1]


def solution(mesh):
    in_specs = (P("col", "row"), P("row", "col"), P("row", "col"), P("col", "row"), P("col", "row"))
    out_specs = (
        P("col", "row"),
        P("col", "row"),
        P("row", "col"),
        P("row", "col"),
        P("col", "row"),
    )
    return jax.shard_map(
        functools.partial(shards, mesh.shape["row"], mesh.shape["col"]),
        mesh=mesh,
        in_specs=in_specs,
        out_specs=out_specs,
        check_vma=False,
    )
```

```python
import functools

import jax
import jax.numpy as jnp
from jax import lax
from jax.experimental import pallas as pl
from jax.experimental.pallas import tpu as pltpu
from jax.sharding import PartitionSpec as P

F32 = jnp.float32
BF16 = jnp.bfloat16
MOST_CHUNKS = 9
KERNEL_VMEM = 24 * 1024 * 1024
ANYWHERE = pl.BlockSpec(memory_space=pl.ANY)


def unit_of(hidden_units):
    return 256 if hidden_units % 256 == 0 else 128


def chunks_of(hidden_units):
    unit = unit_of(hidden_units)
    width = -(-(hidden_units // unit) // MOST_CHUNKS) * unit
    return [(s, min(width, hidden_units - s)) for s in range(0, hidden_units, width)]


def tile_of(width):
    return 256 if width % 256 == 0 else 128


def contract_last(left, right):
    return lax.dot_general(left, right, (((1,), (1,)), ((), ())), preferred_element_type=F32)


def whole(shape):
    return pl.BlockSpec(shape, lambda i: (0,) * len(shape))


class Order:
    def __init__(self):
        self.last = None

    def call(self, kernel, grid, in_specs, out_specs, out_shape, aliases, vmem, cost, name, *args):
        extra = [] if self.last is None or any(self.last is a for a in args) else [self.last]
        extra = [pltpu.with_memory_space_constraint(e, pltpu.HBM) if e.ndim == 2 else e for e in extra]

        def body(*refs):
            kernel(*refs[: len(args)], *refs[len(args) + len(extra) :])

        out = pl.pallas_call(
            body,
            grid=grid,
            in_specs=list(in_specs) + [ANYWHERE] * len(extra),
            out_specs=out_specs,
            out_shape=out_shape,
            input_output_aliases=aliases,
            compiler_params=pltpu.CompilerParams(vmem_limit_bytes=vmem),
            cost_estimate=pl.CostEstimate(flops=cost, bytes_accessed=cost, transcendentals=0),
            name=name,
        )(*args, *extra)
        self.last = out[0]
        return out


def split_store(values, mine_ref, theirs_ref):
    half = mine_ref.shape[1]
    for index, value in enumerate(values):
        mine_ref[index] = value[:half].astype(BF16)
        theirs_ref[index] = value[half:].astype(BF16)


def gate_up_sums(x_ref, gate_ref, up_ref):
    return [
        jnp.dot(x_ref[...], w_ref[...], preferred_element_type=F32) for w_ref in (gate_ref, up_ref)
    ]


def forward_kernel(x_ref, gate_ref, up_ref, c_ref, down_ref, mine_ref, theirs_ref):
    sums = gate_up_sums(x_ref, gate_ref, up_ref)
    split_store(sums + [contract_last(c_ref[...], down_ref[...])], mine_ref, theirs_ref)


def gate_up_kernel(x_ref, gate_ref, up_ref, mine_ref, theirs_ref):
    split_store(gate_up_sums(x_ref, gate_ref, up_ref), mine_ref, theirs_ref)


def back_kernel(c_ref, down_ref, mine_in_ref, theirs_in_ref, mine_ref, theirs_ref):
    split_store([contract_last(c_ref[...], down_ref[...])], mine_ref, theirs_ref)


def forward(order, x, c, weights, start, width, partly=None):
    tokens, depth = (c if x is None else x).shape
    tile = tile_of(width)
    first = start // tile
    half = tokens // 2
    gate, up, down = weights
    part = jax.ShapeDtypeStruct((3, half, width), BF16)
    column = pl.BlockSpec((depth, tile), lambda i: (0, first + i))
    row = pl.BlockSpec((tile, depth), lambda i: (first + i, 0))
    block = whole((tokens, depth))
    if c is None:
        kernel, specs, args = gate_up_kernel, [block, column, column], [x, gate, up]
        piece = pl.BlockSpec((2, half, tile), lambda i: (0, 0, i))
        aliases = {}
    elif x is None:
        kernel, specs, args = back_kernel, [block, row, ANYWHERE, ANYWHERE], [c, down, *partly]
        piece = pl.BlockSpec((1, half, tile), lambda i: (2, 0, i))
        aliases = {2: 0, 3: 1}
    else:
        kernel, specs = forward_kernel, [block, column, column, block, row]
        args = [x, gate, up, c, down]
        piece = pl.BlockSpec((3, half, tile), lambda i: (0, 0, i))
        aliases = {}
    return order.call(
        kernel, (width // tile,), specs, [piece, piece], [part, part], aliases, KERNEL_VMEM, 1000,
        "forward_sums", *args,
    )


def elementwise(order, kernel, name, *args):
    piece = whole(args[0].shape)
    specs = [piece if a.ndim == 3 else pl.BlockSpec(memory_space=pltpu.SMEM) for a in args]
    shape = jax.ShapeDtypeStruct(args[0].shape, BF16)
    return order.call(
        kernel, (1,), specs, [piece], [shape], {}, KERNEL_VMEM, 1000, name, *args
    )[0]


def assemble_kernel(flag_ref, *refs):
    blocks, out_ref = refs[:-1], refs[-1]
    count, rows = len(blocks), blocks[0].shape[0]
    for core in range(2):

        @pl.when(flag_ref[0] == core)
        def _():
            for index, block in enumerate(blocks):
                place = (index + core * (count // 2)) % count
                out_ref[pl.ds(place * rows, rows), :] = block[...]


def assemble(order, flag, blocks):
    rows, depth = blocks[0].shape
    shape = (rows * len(blocks), depth)
    return order.call(
        assemble_kernel, (1,),
        [pl.BlockSpec(memory_space=pltpu.SMEM)] + [whole((rows, depth))] * len(blocks),
        [whole(shape)], [jax.ShapeDtypeStruct(shape, BF16)], {}, KERNEL_VMEM, 1000,
        "assemble_tokens", flag, *blocks,
    )[0]


def transpose_kernel(x_ref, xt_ref):
    xt_ref[...] = x_ref[...].T


def transpose(order, x):
    shape = x.shape[::-1]
    return order.call(
        transpose_kernel, (1,), [whole(x.shape)], [whole(shape)],
        [jax.ShapeDtypeStruct(shape, BF16)], {}, KERNEL_VMEM, 1000, "transpose_tokens", x,
    )[0]


def add_kernel(left_ref, right_ref, out_ref):
    out_ref[...] = (left_ref[...].astype(F32) + right_ref[...].astype(F32)).astype(BF16)


def choose_kernel(left_ref, flag_ref, right_ref, out_ref):
    @pl.when(flag_ref[0] == 0)
    def _():
        out_ref[...] = left_ref[...]

    @pl.when(flag_ref[0] != 0)
    def _():
        out_ref[...] = right_ref[...]


def activation_kernel(left_ref, right_ref, out_ref):
    gate_sum, up_sum, back_sum = (
        left_ref[i].astype(F32) + right_ref[i].astype(F32) for i in range(3)
    )
    sigma = jax.nn.sigmoid(gate_sum)
    silu = gate_sum * sigma
    out_ref[0] = (silu * up_sum).astype(BF16)
    out_ref[1] = (back_sum * up_sum * sigma * (1.0 + gate_sum * (1.0 - sigma))).astype(BF16)
    out_ref[2] = (back_sum * silu).astype(BF16)


def joined(mine_ref, other_ref):
    return [jnp.concatenate([mine_ref[i], other_ref[i]], axis=0) for i in range(3)]


def token_products(acts, weight_refs, before_refs, total_ref):
    gate_ref, up_ref, down_ref = weight_refs
    hidden, gate_act, up_act = acts

    @pl.when(pl.program_id(0) == 0)
    def _():
        if not before_refs:
            total_ref[...] = jnp.zeros_like(total_ref)

    total_ref[0] += jnp.dot(hidden, down_ref[...], preferred_element_type=F32)
    total_ref[1] += contract_last(gate_act, gate_ref[...]) + contract_last(up_act, up_ref[...])


def weight_products(acts, xt_ref, c_ref, grad_gate_ref, grad_up_ref, grad_down_ref):
    hidden, gate_act, up_act = acts
    grad_gate_ref[...] = jnp.dot(xt_ref[...], gate_act, preferred_element_type=F32).astype(BF16)
    grad_up_ref[...] = jnp.dot(xt_ref[...], up_act, preferred_element_type=F32).astype(BF16)
    grad_down_ref[...] = jnp.dot(hidden.T, c_ref[...], preferred_element_type=F32).astype(BF16)


def backward(order, mine, other, xt, c, weights, start, total, grads, parts):
    _, half, width = mine.shape
    tile = tile_of(width)
    first = start // tile
    piece = pl.BlockSpec((3, half, tile), lambda i: (0, 0, i))
    column = pl.BlockSpec((c.shape[1], tile), lambda i: (0, first + i))
    row = pl.BlockSpec((tile, c.shape[1]), lambda i: (first + i, 0))
    resident = pl.BlockSpec(memory_space=pltpu.VMEM)
    with_tokens, with_weights = "tokens" in parts, "weights" in parts
    specs, args, out_specs, shapes, aliases = [piece, piece], [mine, other], [], [], {}
    if with_tokens:
        specs += [column, column, row]
        args += weights
        if total is not None:
            aliases[len(args)] = 0
            specs += [resident]
            args += [total]
        out_specs += [resident]
        shapes += [jax.ShapeDtypeStruct((2,) + c.shape, F32)]
    n_token_args = len(args)
    if with_weights:
        specs += [whole(xt.shape), whole(c.shape)]
        args += [xt, c]
        for index, grad in enumerate(grads or ()):
            aliases[len(args)] = len(out_specs) + index
            specs += [ANYWHERE]
            args += [grad]
        out_specs += [column, column, row]
        shapes += [pltpu.HBM(w.shape, BF16) for w in weights]

    def kernel(*refs):
        ins, outs = refs[: len(args)], refs[len(args) :]
        acts = joined(*ins[:2])
        if with_tokens:
            token_products(acts, ins[2:5], ins[5:n_token_args], outs[0])
        if with_weights:
            weight_products(acts, *ins[n_token_args : n_token_args + 2], *outs[-3:])

    out = order.call(
        kernel, (width // tile,), specs, out_specs, shapes, aliases, KERNEL_VMEM, 1000,
        "backward_products", *args,
    )
    return (out[0] if with_tokens else total), (out[-3:] if with_weights else grads)


def both_cores(pairs):
    return [(2 * a + core, 2 * b + core) for a, b in pairs for core in range(2)]


def shards(n_row, n_col, tokens, gate_weight, up_weight, down_weight, cotangent):
    chips = n_row // 2
    middle = chips // 2
    core = lax.axis_index("row") % 2
    chip = lax.axis_index("row") // 2
    siblings = [(r, r ^ 1) for r in range(n_row)]
    inward = [both_cores([(j, j + 1), (chips - 1 - j, chips - 2 - j)]) for j in range(middle - 1)]
    across = both_cores([(middle - 1, middle), (middle, middle - 1)])
    flags = [
        jnp.where((chip == j) | (chip == chips - 1 - j), 1, 0).astype(jnp.int32).reshape(1)
        for j in range(middle - 1)
    ]
    weights = [
        pltpu.with_memory_space_constraint(w, pltpu.HBM)
        for w in (gate_weight, up_weight, down_weight)
    ]

    order = Order()
    core_flag = core.astype(jnp.int32).reshape(1)

    def travel(block):
        return [block] + [
            lax.ppermute(block, "col", [(s, s ^ j) for s in range(n_col)]) for j in range(1, n_col)
        ]

    token_blocks, cotangent_blocks = travel(tokens), travel(cotangent)
    x = assemble(order, core_flag, token_blocks)

    chunks = chunks_of(gate_weight.shape[1])
    count = len(chunks)
    swapped, partial, arrived, acts, other = {}, {}, {}, {}, {}
    state = [None, None]

    def step_sums(k, partly=None):
        if 0 <= k < count:
            left = x if partly is None else None
            mine, theirs = forward(order, left, c, weights, *chunks[k], partly)
            swapped[k] = (mine, lax.ppermute(theirs, "row", siblings))

    def step_chip(k):
        if 0 <= k < count:
            partial[k] = elementwise(order, add_kernel, "chip_sum", *swapped.pop(k))
            if inward:
                arrived[k] = lax.ppermute(partial[k], "row", inward[0])

    def step_half(k):
        if 0 <= k < count:
            for hop in range(len(inward)):
                partial[k] = elementwise(order, add_kernel, "half_sum", partial[k], arrived[k])
                if hop + 1 < len(inward):
                    arrived[k] = lax.ppermute(partial[k], "row", inward[hop + 1])
            arrived[k] = lax.ppermute(partial[k], "row", across)

    def step_act(k):
        if 0 <= k < count:
            acts[k] = elementwise(
                order, activation_kernel, "activations", partial.pop(k), arrived.pop(k)
            )
            if inward:
                back = [(t, s) for s, t in inward[-1]]
                arrived[k] = lax.ppermute(acts[k], "row", back)

    def step_choose(k):
        if 0 <= k < count:
            for hop in reversed(range(len(inward))):
                acts[k] = elementwise(
                    order, choose_kernel, "choose", acts[k], flags[hop], arrived[k]
                )
                if hop > 0:
                    back = [(t, s) for s, t in inward[hop - 1]]
                    arrived[k] = lax.ppermute(acts[k], "row", back)
            other[k] = lax.ppermute(acts[k], "row", siblings)

    def step_back(k, parts=("tokens", "weights")):
        if 0 <= k < count:
            state[0], state[1] = backward(
                order, acts[k], other[k], xt, c, weights, chunks[k][0], *state, parts
            )

    early = [forward(order, x, None, weights, *chunks[k]) for k in range(2)]
    c = assemble(order, core_flag, cotangent_blocks)
    step_sums(0, early[0])
    step_sums(1, early[1])
    step_chip(0)
    step_chip(1)
    summed = 2
    deferred = [k for k in range(count - 6, count - 3) if k >= 0] + [count - 1]
    for k in range(count):
        fresh = range(summed, min(count, summed + (3 if k == 0 else 2)))
        summed = fresh.stop
        for j in fresh:
            step_sums(j)
        if k == 0:
            xt = transpose(order, x)
        step_half(k)
        step_act(k - 1)
        step_choose(k - 2)
        for j in fresh:
            step_chip(j)
        step_back(k - 3, ("tokens",) if k - 3 in deferred else ("tokens", "weights"))
    for k in deferred[:2]:
        step_back(k, ("weights",))
    step_act(count - 1)
    step_choose(count - 2)
    step_back(count - 3)
    step_back(count - 2)
    step_choose(count - 1)
    step_back(count - 1, ("tokens",))
    total = state[0]

    half = total.shape[1] // 2
    block = total.shape[1] // n_col
    total = total.astype(BF16)
    ordered = jnp.where(
        core == 0, total, jnp.concatenate([total[:, half:], total[:, :half]], axis=1)
    )
    out = ordered[:, :block].astype(F32)
    for j in range(1, n_col):
        piece = ordered[:, j * block : (j + 1) * block]
        out += lax.ppermute(piece, "col", [(s, s ^ j) for s in range(n_col)]).astype(F32)
    out = out.astype(BF16)
    for k in deferred[2:]:
        step_back(k, ("weights",))
    return out[0], out[1], *state[1]


def solution(mesh):
    in_specs = (P("col", "row"), P("row", "col"), P("row", "col"), P("col", "row"), P("col", "row"))
    out_specs = (
        P("col", "row"),
        P("col", "row"),
        P("row", "col"),
        P("row", "col"),
        P("col", "row"),
    )
    return jax.shard_map(
        functools.partial(shards, mesh.shape["row"], mesh.shape["col"]),
        mesh=mesh,
        in_specs=in_specs,
        out_specs=out_specs,
        check_vma=False,
    )
```

```python
import functools

import jax
import jax.numpy as jnp
from jax import lax
from jax.experimental import pallas as pl
from jax.experimental.pallas import tpu as pltpu
from jax.sharding import PartitionSpec as P

F32 = jnp.float32
BF16 = jnp.bfloat16
MOST_CHUNKS = 7
UNIT = 128
TILE = 256
KERNEL_VMEM = 32 * 1024 * 1024
ANYWHERE = pl.BlockSpec(memory_space=pl.ANY)
RESIDENT = pl.BlockSpec(memory_space=pltpu.VMEM)


def chunks_of(hidden_units):
    unit = TILE if hidden_units % TILE == 0 else UNIT
    width = -(-(hidden_units // unit) // MOST_CHUNKS) * unit
    return [(s, min(width, hidden_units - s)) for s in range(0, hidden_units, width)]


def tiles_of(width):
    return [(t, min(TILE, width - t)) for t in range(0, width, TILE)]


def contract_last(left, right):
    return lax.dot_general(left, right, (((1,), (1,)), ((), ())), preferred_element_type=F32)


def whole(shape):
    return pl.BlockSpec(shape, lambda i: (0,) * len(shape))


class Order:
    def __init__(self):
        self.last = None

    def call(self, kernel, grid, in_specs, out_specs, out_shape, aliases, vmem, cost, name, *args,
             scratch=()):
        extra = [] if self.last is None or any(self.last is a for a in args) else [self.last]
        extra = [pltpu.with_memory_space_constraint(e, pltpu.HBM) if e.ndim == 2 else e for e in extra]

        def body(*refs):
            kernel(*refs[: len(args)], *refs[len(args) + len(extra) :])

        out = pl.pallas_call(
            body,
            grid=grid,
            in_specs=list(in_specs) + [ANYWHERE] * len(extra),
            out_specs=out_specs,
            out_shape=out_shape,
            input_output_aliases=aliases,
            scratch_shapes=list(scratch),
            compiler_params=pltpu.CompilerParams(vmem_limit_bytes=vmem),
            cost_estimate=pl.CostEstimate(flops=cost, bytes_accessed=cost // 256, transcendentals=0),
            name=name,
        )(*args, *extra)
        self.last = out[0]
        return out


def split_store(values, mine_ref, theirs_ref):
    half = mine_ref.shape[1]
    for index, value in enumerate(values):
        mine_ref[index] = value[:half].astype(BF16)
        theirs_ref[index] = value[half:].astype(BF16)


def gate_up_sums(x_ref, gate_ref, up_ref):
    return [
        jnp.dot(x_ref[...], w_ref[...], preferred_element_type=F32) for w_ref in (gate_ref, up_ref)
    ]


def forward_kernel(x_ref, gate_ref, up_ref, c_ref, down_ref, mine_ref, theirs_ref):
    sums = gate_up_sums(x_ref, gate_ref, up_ref)
    split_store(sums + [contract_last(c_ref[...], down_ref[...])], mine_ref, theirs_ref)


def gate_up_kernel(x_ref, gate_ref, up_ref, mine_ref, theirs_ref):
    split_store(gate_up_sums(x_ref, gate_ref, up_ref), mine_ref, theirs_ref)


def back_kernel(c_ref, down_ref, mine_in_ref, theirs_in_ref, mine_ref, theirs_ref):
    split_store([contract_last(c_ref[...], down_ref[...])], mine_ref, theirs_ref)


def forward(order, x, c, weights, start, width, partly=None):
    tokens, depth = (c if x is None else x).shape
    tile = TILE if width % TILE == 0 else UNIT
    first = start // tile
    half = tokens // 2
    gate, up, down = weights
    part = jax.ShapeDtypeStruct((3, half, width), BF16)
    column = pl.BlockSpec((depth, tile), lambda i: (0, first + i))
    row = pl.BlockSpec((tile, depth), lambda i: (first + i, 0))
    block = whole((tokens, depth))
    if c is None:
        kernel, specs, args = gate_up_kernel, [block, column, column], [x, gate, up]
        piece = pl.BlockSpec((2, half, tile), lambda i: (0, 0, i))
        aliases = {}
    elif x is None:
        kernel, specs, args = back_kernel, [block, row, ANYWHERE, ANYWHERE], [c, down, *partly]
        piece = pl.BlockSpec((1, half, tile), lambda i: (2, 0, i))
        aliases = {2: 0, 3: 1}
    else:
        kernel, specs = forward_kernel, [block, column, column, block, row]
        args = [x, gate, up, c, down]
        piece = pl.BlockSpec((3, half, tile), lambda i: (0, 0, i))
        aliases = {}
    return order.call(
        kernel, (width // tile,), specs, [piece, piece], [part, part], aliases, KERNEL_VMEM, 1000,
        "forward_sums", *args,
    )


def elementwise(order, kernel, name, *args):
    piece = whole(args[0].shape)
    specs = [piece if a.ndim == 3 else pl.BlockSpec(memory_space=pltpu.SMEM) for a in args]
    shape = jax.ShapeDtypeStruct(args[0].shape, BF16)
    return order.call(
        kernel, (1,), specs, [piece], [shape], {}, KERNEL_VMEM, 1000, name, *args
    )[0]


def assemble_kernel(flag_ref, *refs):
    blocks, out_ref = refs[:-1], refs[-1]
    count, rows = len(blocks), blocks[0].shape[0]
    for core in range(2):

        @pl.when(flag_ref[0] == core)
        def _():
            for index, block in enumerate(blocks):
                place = (index + core * (count // 2)) % count
                out_ref[pl.ds(place * rows, rows), :] = block[...]


def assemble(order, flag, blocks):
    rows, depth = blocks[0].shape
    shape = (rows * len(blocks), depth)
    return order.call(
        assemble_kernel, (1,),
        [pl.BlockSpec(memory_space=pltpu.SMEM)] + [whole((rows, depth))] * len(blocks),
        [whole(shape)], [jax.ShapeDtypeStruct(shape, BF16)], {}, KERNEL_VMEM, 1000,
        "assemble_tokens", flag, *blocks,
    )[0]


def transpose_kernel(x_ref, xt_ref):
    xt_ref[...] = x_ref[...].T


def transpose(order, x):
    shape = x.shape[::-1]
    return order.call(
        transpose_kernel, (1,), [whole(x.shape)], [whole(shape)],
        [jax.ShapeDtypeStruct(shape, BF16)], {}, KERNEL_VMEM, 1000, "transpose_tokens", x,
    )[0]


def add_kernel(left_ref, right_ref, out_ref):
    out_ref[...] = (left_ref[...].astype(F32) + right_ref[...].astype(F32)).astype(BF16)


def choose_kernel(left_ref, flag_ref, right_ref, out_ref):
    @pl.when(flag_ref[0] == 0)
    def _():
        out_ref[...] = left_ref[...]

    @pl.when(flag_ref[0] != 0)
    def _():
        out_ref[...] = right_ref[...]


def activation_kernel(left_ref, right_ref, out_ref):
    gate_sum, up_sum, back_sum = (
        left_ref[i].astype(F32) + right_ref[i].astype(F32) for i in range(3)
    )
    sigma = jax.nn.sigmoid(gate_sum)
    silu = gate_sum * sigma
    out_ref[0] = (silu * up_sum).astype(BF16)
    out_ref[1] = (back_sum * up_sum * sigma * (1.0 + gate_sum * (1.0 - sigma))).astype(BF16)
    out_ref[2] = (back_sum * silu).astype(BF16)


def backward(order, mine, other, xt, c, weights, start, total, grads, parts):
    _, half, width = mine.shape
    tokens, depth = c.shape
    tiles = tiles_of(width)
    with_tokens, with_weights = "tokens" in parts, "weights" in parts
    piece = whole(mine.shape)
    specs, args, out_specs, shapes, aliases = [piece, piece], [mine, other], [], [], {}
    if with_tokens:
        specs += [ANYWHERE] * 3
        args += weights
        if total is not None:
            aliases[len(args)] = 0
            specs += [RESIDENT]
            args += [total]
        out_specs += [RESIDENT]
        shapes += [jax.ShapeDtypeStruct((2,) + c.shape, F32)]
    n_token_args = len(args)
    if with_weights:
        specs += [whole(xt.shape), whole(c.shape)]
        args += [xt, c]
        for index, grad in enumerate(grads or ()):
            aliases[len(args)] = len(out_specs) + index
            specs += [ANYWHERE]
            args += [grad]
        out_specs += [ANYWHERE] * 3
        shapes += [pltpu.HBM(w.shape, BF16) for w in weights]
    slab = [
        pltpu.VMEM((depth, width), BF16),
        pltpu.VMEM((depth, width), BF16),
        pltpu.VMEM((width, depth), BF16),
    ]
    scratch = [pltpu.VMEM((3, tokens, width), BF16)]
    scratch += (slab + [pltpu.SemaphoreType.DMA((3,))]) if with_tokens else []
    scratch += (slab + [pltpu.SemaphoreType.DMA((len(tiles), 3))]) if with_weights else []

    def kernel(*refs):
        ins = refs[: len(args)]
        outs = refs[len(args) : len(args) + len(shapes)]
        acts, *buffers = refs[len(args) + len(shapes) :]
        fetches, stores = [], []
        if with_tokens:
            whole_chunk = pl.ds(start, width)
            sources = [ins[2].at[:, whole_chunk], ins[3].at[:, whole_chunk], ins[4].at[whole_chunk]]
            fetches = [
                pltpu.make_async_copy(source, buffers[i], buffers[3].at[i])
                for i, source in enumerate(sources)
            ]
            for i in (2, 0, 1):
                fetches[i].start()
        for i in range(3):
            acts[i, :half] = ins[0][i]
            acts[i, half:] = ins[1][i]
        if with_weights:
            xt_ref, c_ref = ins[n_token_args : n_token_args + 2]
            *staged, sem = buffers[-4:]
            for number, (at, size) in enumerate(tiles):
                here, there = pl.ds(at, size), pl.ds(start + at, size)
                for i in range(3):
                    if i < 2:
                        value = jnp.dot(
                            xt_ref[...], acts[i + 1, :, here], preferred_element_type=F32
                        )
                        source, target = staged[i].at[:, here], outs[i - 3].at[:, there]
                    else:
                        value = jnp.dot(
                            acts[0, :, here].T, c_ref[...], preferred_element_type=F32
                        )
                        source, target = staged[i].at[here], outs[i - 3].at[there]
                    source[...] = value.astype(BF16)
                    stores.append(pltpu.make_async_copy(source, target, sem.at[number, i]))
                    stores[-1].start()
        if with_tokens:
            total_ref = outs[0]
            fetches[2].wait()
            mixed = jnp.dot(acts[0], buffers[2][...], preferred_element_type=F32)
            total_ref[0] = mixed if total is None else total_ref[0] + mixed
            fetches[0].wait()
            fetches[1].wait()
            inputs = contract_last(acts[1], buffers[0][...]) + contract_last(
                acts[2], buffers[1][...]
            )
            total_ref[1] = inputs if total is None else total_ref[1] + inputs
        for store in stores:
            store.wait()

    cost = 1000 if with_tokens else 6 * tokens * depth * width
    out = order.call(
        kernel, (1,), specs, out_specs, shapes, aliases, KERNEL_VMEM, cost,
        "backward_products", *args, scratch=scratch,
    )
    return (out[0] if with_tokens else total), (out[-3:] if with_weights else grads)


def both_cores(pairs):
    return [(2 * a + core, 2 * b + core) for a, b in pairs for core in range(2)]


def shards(n_row, n_col, tokens, gate_weight, up_weight, down_weight, cotangent):
    chips = n_row // 2
    middle = chips // 2
    core = lax.axis_index("row") % 2
    chip = lax.axis_index("row") // 2
    siblings = [(r, r ^ 1) for r in range(n_row)]
    inward = [both_cores([(j, j + 1), (chips - 1 - j, chips - 2 - j)]) for j in range(middle - 1)]
    across = both_cores([(middle - 1, middle), (middle, middle - 1)])
    flags = [
        jnp.where((chip == j) | (chip == chips - 1 - j), 1, 0).astype(jnp.int32).reshape(1)
        for j in range(middle - 1)
    ]
    weights = [
        pltpu.with_memory_space_constraint(w, pltpu.HBM)
        for w in (gate_weight, up_weight, down_weight)
    ]

    order = Order()
    core_flag = core.astype(jnp.int32).reshape(1)

    def travel(block):
        return [block] + [
            lax.ppermute(block, "col", [(s, s ^ j) for s in range(n_col)]) for j in range(1, n_col)
        ]

    token_blocks, cotangent_blocks = travel(tokens), travel(cotangent)
    x = assemble(order, core_flag, token_blocks)

    chunks = chunks_of(gate_weight.shape[1])
    count = len(chunks)
    swapped, partial, arrived, acts, other = {}, {}, {}, {}, {}
    state = [None, None]

    def step_sums(k, partly=None):
        if 0 <= k < count:
            left = x if partly is None else None
            mine, theirs = forward(order, left, c, weights, *chunks[k], partly)
            swapped[k] = (mine, lax.ppermute(theirs, "row", siblings))

    def step_chip(k):
        if 0 <= k < count:
            partial[k] = elementwise(order, add_kernel, "chip_sum", *swapped.pop(k))
            if inward:
                arrived[k] = lax.ppermute(partial[k], "row", inward[0])

    def step_half(k):
        if 0 <= k < count:
            for hop in range(len(inward)):
                partial[k] = elementwise(order, add_kernel, "half_sum", partial[k], arrived[k])
                if hop + 1 < len(inward):
                    arrived[k] = lax.ppermute(partial[k], "row", inward[hop + 1])
            arrived[k] = lax.ppermute(partial[k], "row", across)

    def step_act(k):
        if 0 <= k < count:
            acts[k] = elementwise(
                order, activation_kernel, "activations", partial.pop(k), arrived.pop(k)
            )
            if inward:
                back = [(t, s) for s, t in inward[-1]]
                arrived[k] = lax.ppermute(acts[k], "row", back)

    def step_choose(k):
        if 0 <= k < count:
            for hop in reversed(range(len(inward))):
                acts[k] = elementwise(
                    order, choose_kernel, "choose", acts[k], flags[hop], arrived[k]
                )
                if hop > 0:
                    back = [(t, s) for s, t in inward[hop - 1]]
                    arrived[k] = lax.ppermute(acts[k], "row", back)
            other[k] = lax.ppermute(acts[k], "row", siblings)

    def step_back(k, parts=("tokens", "weights")):
        if 0 <= k < count:
            state[0], state[1] = backward(
                order, acts[k], other[k], xt, c, weights, chunks[k][0], *state, parts
            )

    early = [forward(order, x, None, weights, *chunks[k]) for k in range(2)]
    c = assemble(order, core_flag, cotangent_blocks)
    step_sums(0, early[0])
    step_sums(1, early[1])
    step_chip(0)
    step_chip(1)
    summed = 2
    deferred = [k for k in range(count - 6, count - 3) if k >= 0] + [count - 1]
    for k in range(count):
        fresh = range(summed, min(count, summed + (3 if k == 0 else 2)))
        summed = fresh.stop
        for j in fresh:
            step_sums(j)
        if k == 0:
            xt = transpose(order, x)
        step_half(k)
        step_act(k - 1)
        step_choose(k - 2)
        for j in fresh:
            step_chip(j)
        step_back(k - 3, ("tokens",) if k - 3 in deferred else ("tokens", "weights"))
    for k in deferred[:1]:
        step_back(k, ("weights",))
    step_act(count - 1)
    for k in deferred[1:2]:
        step_back(k, ("weights",))
    step_choose(count - 2)
    step_back(count - 3)
    step_back(count - 2)
    step_choose(count - 1)
    step_back(count - 1, ("tokens",))
    total = state[0]

    half = total.shape[1] // 2
    block = total.shape[1] // n_col
    total = total.astype(BF16)
    ordered = jnp.where(
        core == 0, total, jnp.concatenate([total[:, half:], total[:, :half]], axis=1)
    )
    out = ordered[:, :block].astype(F32)
    for j in range(1, n_col):
        piece = ordered[:, j * block : (j + 1) * block]
        out += lax.ppermute(piece, "col", [(s, s ^ j) for s in range(n_col)]).astype(F32)
    out = out.astype(BF16)
    for k in deferred[2:]:
        step_back(k, ("weights",))
    return out[0], out[1], *state[1]


def solution(mesh):
    in_specs = (P("col", "row"), P("row", "col"), P("row", "col"), P("col", "row"), P("col", "row"))
    out_specs = (
        P("col", "row"),
        P("col", "row"),
        P("row", "col"),
        P("row", "col"),
        P("col", "row"),
    )
    return jax.shard_map(
        functools.partial(shards, mesh.shape["row"], mesh.shape["col"]),
        mesh=mesh,
        in_specs=in_specs,
        out_specs=out_specs,
        check_vma=False,
    )
```

```python
import functools

import jax
import jax.numpy as jnp
from jax import lax
from jax.experimental import pallas as pl
from jax.experimental.pallas import tpu as pltpu
from jax.sharding import PartitionSpec as P

F32 = jnp.float32
BF16 = jnp.bfloat16
MOST_CHUNKS = 7
UNIT = 128
TILE = 256
KERNEL_VMEM = 32 * 1024 * 1024
ANYWHERE = pl.BlockSpec(memory_space=pl.ANY)
RESIDENT = pl.BlockSpec(memory_space=pltpu.VMEM)


def chunks_of(hidden_units):
    unit = TILE if hidden_units % TILE == 0 else UNIT
    width = -(-(hidden_units // unit) // MOST_CHUNKS) * unit
    return [(s, min(width, hidden_units - s)) for s in range(0, hidden_units, width)]


def tiles_of(width):
    return [(t, min(TILE, width - t)) for t in range(0, width, TILE)]


def contract_last(left, right):
    return lax.dot_general(left, right, (((1,), (1,)), ((), ())), preferred_element_type=F32)


def whole(shape):
    return pl.BlockSpec(shape, lambda i: (0,) * len(shape))


class Order:
    def __init__(self):
        self.last = None

    def call(self, kernel, grid, in_specs, out_specs, out_shape, aliases, vmem, cost, name, *args,
             scratch=()):
        extra = [] if self.last is None or any(self.last is a for a in args) else [self.last]
        extra = [pltpu.with_memory_space_constraint(e, pltpu.HBM) if e.ndim == 2 else e for e in extra]

        def body(*refs):
            kernel(*refs[: len(args)], *refs[len(args) + len(extra) :])

        out = pl.pallas_call(
            body,
            grid=grid,
            in_specs=list(in_specs) + [ANYWHERE] * len(extra),
            out_specs=out_specs,
            out_shape=out_shape,
            input_output_aliases=aliases,
            scratch_shapes=list(scratch),
            compiler_params=pltpu.CompilerParams(vmem_limit_bytes=vmem),
            cost_estimate=pl.CostEstimate(flops=cost, bytes_accessed=cost // 256, transcendentals=0),
            name=name,
        )(*args, *extra)
        self.last = out[0]
        return out


def split_store(values, mine_ref, theirs_ref):
    half = mine_ref.shape[1]
    for index, value in enumerate(values):
        mine_ref[index] = value[:half].astype(BF16)
        theirs_ref[index] = value[half:].astype(BF16)


def gate_up_sums(x_ref, gate_ref, up_ref):
    return [
        jnp.dot(x_ref[...], w_ref[...], preferred_element_type=F32) for w_ref in (gate_ref, up_ref)
    ]


def forward_kernel(x_ref, gate_ref, up_ref, c_ref, down_ref, mine_ref, theirs_ref):
    sums = gate_up_sums(x_ref, gate_ref, up_ref)
    split_store(sums + [contract_last(c_ref[...], down_ref[...])], mine_ref, theirs_ref)


def gate_up_kernel(x_ref, gate_ref, up_ref, mine_ref, theirs_ref):
    split_store(gate_up_sums(x_ref, gate_ref, up_ref), mine_ref, theirs_ref)


def back_kernel(c_ref, down_ref, mine_in_ref, theirs_in_ref, mine_ref, theirs_ref):
    split_store([contract_last(c_ref[...], down_ref[...])], mine_ref, theirs_ref)


def forward(order, x, c, weights, start, width, partly=None):
    tokens, depth = (c if x is None else x).shape
    tile = TILE if width % TILE == 0 else UNIT
    first = start // tile
    half = tokens // 2
    gate, up, down = weights
    part = jax.ShapeDtypeStruct((3, half, width), BF16)
    column = pl.BlockSpec((depth, tile), lambda i: (0, first + i))
    row = pl.BlockSpec((tile, depth), lambda i: (first + i, 0))
    block = whole((tokens, depth))
    if c is None:
        kernel, specs, args = gate_up_kernel, [block, column, column], [x, gate, up]
        piece = pl.BlockSpec((2, half, tile), lambda i: (0, 0, i))
        aliases = {}
    elif x is None:
        kernel, specs, args = back_kernel, [block, row, ANYWHERE, ANYWHERE], [c, down, *partly]
        piece = pl.BlockSpec((1, half, tile), lambda i: (2, 0, i))
        aliases = {2: 0, 3: 1}
    else:
        kernel, specs = forward_kernel, [block, column, column, block, row]
        args = [x, gate, up, c, down]
        piece = pl.BlockSpec((3, half, tile), lambda i: (0, 0, i))
        aliases = {}
    return order.call(
        kernel, (width // tile,), specs, [piece, piece], [part, part], aliases, KERNEL_VMEM, 1000,
        "forward_sums", *args,
    )


def elementwise(order, kernel, name, *args):
    piece = whole(args[0].shape)
    specs = [piece if a.ndim == 3 else pl.BlockSpec(memory_space=pltpu.SMEM) for a in args]
    shape = jax.ShapeDtypeStruct(args[0].shape, BF16)
    return order.call(
        kernel, (1,), specs, [piece], [shape], {}, KERNEL_VMEM, 1000, name, *args
    )[0]


def assemble_kernel(flag_ref, *refs):
    blocks, out_ref = refs[:-1], refs[-1]
    count, rows = len(blocks), blocks[0].shape[0]
    for core in range(2):

        @pl.when(flag_ref[0] == core)
        def _():
            for index, block in enumerate(blocks):
                place = (index + core * (count // 2)) % count
                out_ref[pl.ds(place * rows, rows), :] = block[...]


def assemble(order, flag, blocks):
    rows, depth = blocks[0].shape
    shape = (rows * len(blocks), depth)
    return order.call(
        assemble_kernel, (1,),
        [pl.BlockSpec(memory_space=pltpu.SMEM)] + [whole((rows, depth))] * len(blocks),
        [whole(shape)], [jax.ShapeDtypeStruct(shape, BF16)], {}, KERNEL_VMEM, 1000,
        "assemble_tokens", flag, *blocks,
    )[0]


def transpose_kernel(x_ref, xt_ref):
    xt_ref[...] = x_ref[...].T


def transpose(order, x):
    shape = x.shape[::-1]
    return order.call(
        transpose_kernel, (1,), [whole(x.shape)], [whole(shape)],
        [jax.ShapeDtypeStruct(shape, BF16)], {}, KERNEL_VMEM, 1000, "transpose_tokens", x,
    )[0]


def add_kernel(left_ref, right_ref, out_ref):
    out_ref[...] = (left_ref[...].astype(F32) + right_ref[...].astype(F32)).astype(BF16)


def choose_kernel(left_ref, flag_ref, right_ref, out_ref):
    @pl.when(flag_ref[0] == 0)
    def _():
        out_ref[...] = left_ref[...]

    @pl.when(flag_ref[0] != 0)
    def _():
        out_ref[...] = right_ref[...]


def activation_kernel(left_ref, right_ref, out_ref):
    gate_sum, up_sum, back_sum = (
        left_ref[i].astype(F32) + right_ref[i].astype(F32) for i in range(3)
    )
    sigma = jax.nn.sigmoid(gate_sum)
    silu = gate_sum * sigma
    out_ref[0] = (silu * up_sum).astype(BF16)
    out_ref[1] = (back_sum * up_sum * sigma * (1.0 + gate_sum * (1.0 - sigma))).astype(BF16)
    out_ref[2] = (back_sum * silu).astype(BF16)


def backward(order, mine, other, xt, c, weights, start, total, grads, parts):
    _, half, width = mine.shape
    tokens, depth = c.shape
    tiles = tiles_of(width)
    with_tokens, with_weights = "tokens" in parts, "weights" in parts
    piece = whole(mine.shape)
    specs, args, out_specs, shapes, aliases = [piece, piece], [mine, other], [], [], {}
    if with_tokens:
        specs += [ANYWHERE] * 3
        args += weights
        if total is not None:
            aliases[len(args)] = 0
            specs += [RESIDENT]
            args += [total]
        out_specs += [RESIDENT]
        shapes += [jax.ShapeDtypeStruct((2,) + c.shape, F32)]
    n_token_args = len(args)
    if with_weights:
        specs += [whole(xt.shape), whole(c.shape)]
        args += [xt, c]
        for index, grad in enumerate(grads or ()):
            aliases[len(args)] = len(out_specs) + index
            specs += [ANYWHERE]
            args += [grad]
        out_specs += [ANYWHERE] * 3
        shapes += [pltpu.HBM(w.shape, BF16) for w in weights]
    slab = [
        pltpu.VMEM((depth, width), BF16),
        pltpu.VMEM((depth, width), BF16),
        pltpu.VMEM((width, depth), BF16),
    ]
    scratch = [pltpu.VMEM((3, tokens, width), BF16)]
    scratch += (slab + [pltpu.SemaphoreType.DMA((3,))]) if with_tokens else []
    scratch += (slab + [pltpu.SemaphoreType.DMA((len(tiles), 3))]) if with_weights else []

    def kernel(*refs):
        ins = refs[: len(args)]
        outs = refs[len(args) : len(args) + len(shapes)]
        acts, *buffers = refs[len(args) + len(shapes) :]
        fetches, stores = [], []
        if with_tokens:
            whole_chunk = pl.ds(start, width)
            sources = [ins[2].at[:, whole_chunk], ins[3].at[:, whole_chunk], ins[4].at[whole_chunk]]
            fetches = [
                pltpu.make_async_copy(source, buffers[i], buffers[3].at[i])
                for i, source in enumerate(sources)
            ]
            for i in (2, 0, 1):
                fetches[i].start()
        for i in range(3):
            acts[i, :half] = ins[0][i]
            acts[i, half:] = ins[1][i]
        if with_weights:
            xt_ref, c_ref = ins[n_token_args : n_token_args + 2]
            *staged, sem = buffers[-4:]
            for number, (at, size) in enumerate(tiles):
                here, there = pl.ds(at, size), pl.ds(start + at, size)
                for i in range(3):
                    if i < 2:
                        value = jnp.dot(
                            xt_ref[...], acts[i + 1, :, here], preferred_element_type=F32
                        )
                        source, target = staged[i].at[:, here], outs[i - 3].at[:, there]
                    else:
                        value = jnp.dot(
                            acts[0, :, here].T, c_ref[...], preferred_element_type=F32
                        )
                        source, target = staged[i].at[here], outs[i - 3].at[there]
                    source[...] = value.astype(BF16)
                    stores.append(pltpu.make_async_copy(source, target, sem.at[number, i]))
                    stores[-1].start()
        if with_tokens:
            total_ref = outs[0]
            fetches[2].wait()
            mixed = jnp.dot(acts[0], buffers[2][...], preferred_element_type=F32)
            total_ref[0] = mixed if total is None else total_ref[0] + mixed
            fetches[0].wait()
            fetches[1].wait()
            inputs = contract_last(acts[1], buffers[0][...]) + contract_last(
                acts[2], buffers[1][...]
            )
            total_ref[1] = inputs if total is None else total_ref[1] + inputs
        for store in stores:
            store.wait()

    out = order.call(
        kernel, (1,), specs, out_specs, shapes, aliases, KERNEL_VMEM, 1000,
        "backward_products", *args, scratch=scratch,
    )
    return (out[0] if with_tokens else total), (out[-3:] if with_weights else grads)


def both_cores(pairs):
    return [(2 * a + core, 2 * b + core) for a, b in pairs for core in range(2)]


def shards(n_row, n_col, tokens, gate_weight, up_weight, down_weight, cotangent):
    chips = n_row // 2
    middle = chips // 2
    core = lax.axis_index("row") % 2
    chip = lax.axis_index("row") // 2
    siblings = [(r, r ^ 1) for r in range(n_row)]
    inward = [both_cores([(j, j + 1), (chips - 1 - j, chips - 2 - j)]) for j in range(middle - 1)]
    across = both_cores([(middle - 1, middle), (middle, middle - 1)])
    flags = [
        jnp.where((chip == j) | (chip == chips - 1 - j), 1, 0).astype(jnp.int32).reshape(1)
        for j in range(middle - 1)
    ]
    weights = [
        pltpu.with_memory_space_constraint(w, pltpu.HBM)
        for w in (gate_weight, up_weight, down_weight)
    ]

    order = Order()
    core_flag = core.astype(jnp.int32).reshape(1)

    def travel(block):
        return [block] + [
            lax.ppermute(block, "col", [(s, s ^ j) for s in range(n_col)]) for j in range(1, n_col)
        ]

    token_blocks, cotangent_blocks = travel(tokens), travel(cotangent)
    x = assemble(order, core_flag, token_blocks)

    chunks = chunks_of(gate_weight.shape[1])
    count = len(chunks)
    swapped, partial, arrived, acts, other = {}, {}, {}, {}, {}
    state = [None, None]

    def step_sums(k, partly=None):
        if 0 <= k < count:
            left = x if partly is None else None
            mine, theirs = forward(order, left, c, weights, *chunks[k], partly)
            swapped[k] = (mine, lax.ppermute(theirs, "row", siblings))

    def step_chip(k):
        if 0 <= k < count:
            partial[k] = elementwise(order, add_kernel, "chip_sum", *swapped.pop(k))
            if inward:
                arrived[k] = lax.ppermute(partial[k], "row", inward[0])

    def step_half(k):
        if 0 <= k < count:
            for hop in range(len(inward)):
                partial[k] = elementwise(order, add_kernel, "half_sum", partial[k], arrived[k])
                if hop + 1 < len(inward):
                    arrived[k] = lax.ppermute(partial[k], "row", inward[hop + 1])
            arrived[k] = lax.ppermute(partial[k], "row", across)

    def step_act(k):
        if 0 <= k < count:
            acts[k] = elementwise(
                order, activation_kernel, "activations", partial.pop(k), arrived.pop(k)
            )
            if inward:
                back = [(t, s) for s, t in inward[-1]]
                arrived[k] = lax.ppermute(acts[k], "row", back)

    def step_choose(k):
        if 0 <= k < count:
            for hop in reversed(range(len(inward))):
                acts[k] = elementwise(
                    order, choose_kernel, "choose", acts[k], flags[hop], arrived[k]
                )
                if hop > 0:
                    back = [(t, s) for s, t in inward[hop - 1]]
                    arrived[k] = lax.ppermute(acts[k], "row", back)
            other[k] = lax.ppermute(acts[k], "row", siblings)

    def step_back(k, parts=("tokens", "weights")):
        if 0 <= k < count:
            state[0], state[1] = backward(
                order, acts[k], other[k], xt, c, weights, chunks[k][0], *state, parts
            )

    early = [forward(order, x, None, weights, *chunks[k]) for k in range(2)]
    c = assemble(order, core_flag, cotangent_blocks)
    step_sums(0, early[0])
    step_sums(1, early[1])
    step_chip(0)
    step_chip(1)
    summed = 2
    for k in range(count):
        fresh = range(summed, min(count, summed + (3 if k == 0 else 2)))
        summed = fresh.stop
        for j in fresh:
            step_sums(j)
        if k == 0:
            xt = transpose(order, x)
        step_half(k)
        step_act(k - 1)
        step_choose(k - 2)
        for j in fresh:
            step_chip(j)
        step_back(k - 3, ("tokens",) if k == count - 2 else ("tokens", "weights"))
    step_act(count - 1)
    step_back(count - 5, ("weights",))
    step_choose(count - 2)
    step_back(count - 3, ("tokens",))
    step_choose(count - 1)
    step_back(count - 2, ("tokens",))
    step_back(count - 1, ("tokens",))
    total = state[0]

    half = total.shape[1] // 2
    block = total.shape[1] // n_col
    total = total.astype(BF16)
    ordered = jnp.where(
        core == 0, total, jnp.concatenate([total[:, half:], total[:, :half]], axis=1)
    )
    out = ordered[:, :block].astype(F32)
    for j in range(1, n_col):
        piece = ordered[:, j * block : (j + 1) * block]
        out += lax.ppermute(piece, "col", [(s, s ^ j) for s in range(n_col)]).astype(F32)
    out = out.astype(BF16)
    for k in range(count - 3, count):
        step_back(k, ("weights",))
    return out[0], out[1], *state[1]


def solution(mesh):
    in_specs = (P("col", "row"), P("row", "col"), P("row", "col"), P("col", "row"), P("col", "row"))
    out_specs = (
        P("col", "row"),
        P("col", "row"),
        P("row", "col"),
        P("row", "col"),
        P("col", "row"),
    )
    return jax.shard_map(
        functools.partial(shards, mesh.shape["row"], mesh.shape["col"]),
        mesh=mesh,
        in_specs=in_specs,
        out_specs=out_specs,
        check_vma=False,
    )
```

```python
import functools

import jax
import jax.numpy as jnp
from jax import lax
from jax.experimental import pallas as pl
from jax.experimental.pallas import tpu as pltpu
from jax.sharding import PartitionSpec as P

F32 = jnp.float32
BF16 = jnp.bfloat16
MOST_CHUNKS = 9
UNIT = 128
TILE = 256
KERNEL_VMEM = 24 * 1024 * 1024
ANYWHERE = pl.BlockSpec(memory_space=pl.ANY)
RESIDENT = pl.BlockSpec(memory_space=pltpu.VMEM)


def chunks_of(hidden_units):
    unit = TILE if hidden_units % TILE == 0 else UNIT
    width = -(-(hidden_units // unit) // MOST_CHUNKS) * unit
    return [(s, min(width, hidden_units - s)) for s in range(0, hidden_units, width)]


def tiles_of(width):
    return [(t, min(TILE, width - t)) for t in range(0, width, TILE)]


def contract_last(left, right):
    return lax.dot_general(left, right, (((1,), (1,)), ((), ())), preferred_element_type=F32)


def whole(shape):
    return pl.BlockSpec(shape, lambda i: (0,) * len(shape))


class Order:
    def __init__(self):
        self.last = None

    def call(self, kernel, grid, in_specs, out_specs, out_shape, aliases, vmem, cost, name, *args,
             scratch=()):
        extra = [] if self.last is None or any(self.last is a for a in args) else [self.last]
        extra = [pltpu.with_memory_space_constraint(e, pltpu.HBM) if e.ndim == 2 else e for e in extra]

        def body(*refs):
            kernel(*refs[: len(args)], *refs[len(args) + len(extra) :])

        out = pl.pallas_call(
            body,
            grid=grid,
            in_specs=list(in_specs) + [ANYWHERE] * len(extra),
            out_specs=out_specs,
            out_shape=out_shape,
            input_output_aliases=aliases,
            scratch_shapes=list(scratch),
            compiler_params=pltpu.CompilerParams(vmem_limit_bytes=vmem),
            cost_estimate=pl.CostEstimate(flops=cost, bytes_accessed=cost // 256, transcendentals=0),
            name=name,
        )(*args, *extra)
        self.last = out[0]
        return out


def split_store(values, mine_ref, theirs_ref):
    half = mine_ref.shape[1]
    for index, value in enumerate(values):
        mine_ref[index] = value[:half].astype(BF16)
        theirs_ref[index] = value[half:].astype(BF16)


def gate_up_sums(x_ref, gate_ref, up_ref):
    return [
        jnp.dot(x_ref[...], w_ref[...], preferred_element_type=F32) for w_ref in (gate_ref, up_ref)
    ]


def forward_kernel(x_ref, gate_ref, up_ref, c_ref, down_ref, mine_ref, theirs_ref):
    sums = gate_up_sums(x_ref, gate_ref, up_ref)
    split_store(sums + [contract_last(c_ref[...], down_ref[...])], mine_ref, theirs_ref)


def gate_up_kernel(x_ref, gate_ref, up_ref, mine_ref, theirs_ref):
    split_store(gate_up_sums(x_ref, gate_ref, up_ref), mine_ref, theirs_ref)


def back_kernel(c_ref, down_ref, mine_in_ref, theirs_in_ref, mine_ref, theirs_ref):
    split_store([contract_last(c_ref[...], down_ref[...])], mine_ref, theirs_ref)


def forward(order, x, c, weights, start, width, partly=None):
    tokens, depth = (c if x is None else x).shape
    tile = TILE if width % TILE == 0 else UNIT
    first = start // tile
    half = tokens // 2
    gate, up, down = weights
    part = pltpu.VMEM((3, half, width), BF16)
    column = pl.BlockSpec((depth, tile), lambda i: (0, first + i))
    row = pl.BlockSpec((tile, depth), lambda i: (first + i, 0))
    block = whole((tokens, depth))
    if c is None:
        kernel, specs, args = gate_up_kernel, [block, column, column], [x, gate, up]
        piece = pl.BlockSpec((2, half, tile), lambda i: (0, 0, i))
        aliases = {}
    elif x is None:
        kernel, specs, args = back_kernel, [block, row, ANYWHERE, ANYWHERE], [c, down, *partly]
        piece = pl.BlockSpec((1, half, tile), lambda i: (2, 0, i))
        aliases = {2: 0, 3: 1}
    else:
        kernel, specs = forward_kernel, [block, column, column, block, row]
        args = [x, gate, up, c, down]
        piece = pl.BlockSpec((3, half, tile), lambda i: (0, 0, i))
        aliases = {}
    return order.call(
        kernel, (width // tile,), specs, [piece, piece], [part, part], aliases, KERNEL_VMEM, 1000,
        "forward_sums", *args,
    )


def elementwise(order, kernel, name, *args):
    piece = whole(args[0].shape)
    specs = [piece if a.ndim == 3 else pl.BlockSpec(memory_space=pltpu.SMEM) for a in args]
    shape = pltpu.VMEM(args[0].shape, BF16)
    return order.call(
        kernel, (1,), specs, [piece], [shape], {}, KERNEL_VMEM, 1000, name, *args
    )[0]


def assemble_kernel(flag_ref, *refs):
    blocks, out_ref = refs[:-1], refs[-1]
    count, rows = len(blocks), blocks[0].shape[0]
    for core in range(2):

        @pl.when(flag_ref[0] == core)
        def _():
            for index, block in enumerate(blocks):
                place = (index + core * (count // 2)) % count
                out_ref[pl.ds(place * rows, rows), :] = block[...]


def assemble(order, flag, blocks):
    rows, depth = blocks[0].shape
    shape = (rows * len(blocks), depth)
    return order.call(
        assemble_kernel, (1,),
        [pl.BlockSpec(memory_space=pltpu.SMEM)] + [whole((rows, depth))] * len(blocks),
        [whole(shape)], [jax.ShapeDtypeStruct(shape, BF16)], {}, KERNEL_VMEM, 1000,
        "assemble_tokens", flag, *blocks,
    )[0]


def transpose_kernel(x_ref, xt_ref):
    xt_ref[...] = x_ref[...].T


def transpose(order, x):
    shape = x.shape[::-1]
    return order.call(
        transpose_kernel, (1,), [whole(x.shape)], [whole(shape)],
        [jax.ShapeDtypeStruct(shape, BF16)], {}, KERNEL_VMEM, 1000, "transpose_tokens", x,
    )[0]


def add_kernel(left_ref, right_ref, out_ref):
    out_ref[...] = (left_ref[...].astype(F32) + right_ref[...].astype(F32)).astype(BF16)


def choose_kernel(left_ref, flag_ref, right_ref, out_ref):
    @pl.when(flag_ref[0] == 0)
    def _():
        out_ref[...] = left_ref[...]

    @pl.when(flag_ref[0] != 0)
    def _():
        out_ref[...] = right_ref[...]


def activation_kernel(left_ref, right_ref, out_ref):
    gate_sum, up_sum, back_sum = (
        left_ref[i].astype(F32) + right_ref[i].astype(F32) for i in range(3)
    )
    sigma = jax.nn.sigmoid(gate_sum)
    silu = gate_sum * sigma
    out_ref[0] = (silu * up_sum).astype(BF16)
    out_ref[1] = (back_sum * up_sum * sigma * (1.0 + gate_sum * (1.0 - sigma))).astype(BF16)
    out_ref[2] = (back_sum * silu).astype(BF16)


def backward(order, mine, other, xt, c, weights, start, total, grads, parts):
    _, half, width = mine.shape
    tokens, depth = c.shape
    tiles = tiles_of(width)
    with_tokens, with_weights = "tokens" in parts, "weights" in parts
    piece = whole(mine.shape)
    specs, args, out_specs, shapes, aliases = [piece, piece], [mine, other], [], [], {}
    if with_tokens:
        specs += [ANYWHERE] * 3
        args += weights
        if total is not None:
            aliases[len(args)] = 0
            specs += [RESIDENT]
            args += [total]
        out_specs += [RESIDENT]
        shapes += [jax.ShapeDtypeStruct((2,) + c.shape, F32)]
    n_token_args = len(args)
    if with_weights:
        specs += [whole(xt.shape), whole(c.shape)]
        args += [xt, c]
        for index, grad in enumerate(grads or ()):
            aliases[len(args)] = len(out_specs) + index
            specs += [ANYWHERE]
            args += [grad]
        out_specs += [ANYWHERE] * 3
        shapes += [pltpu.HBM(w.shape, BF16) for w in weights]
    slab = [
        pltpu.VMEM((depth, width), BF16),
        pltpu.VMEM((depth, width), BF16),
        pltpu.VMEM((width, depth), BF16),
    ]
    scratch = [pltpu.VMEM((3, tokens, width), BF16)]
    scratch += (slab + [pltpu.SemaphoreType.DMA((3,))]) if with_tokens else []
    scratch += (slab + [pltpu.SemaphoreType.DMA((len(tiles), 3))]) if with_weights else []

    def kernel(*refs):
        ins = refs[: len(args)]
        outs = refs[len(args) : len(args) + len(shapes)]
        acts, *buffers = refs[len(args) + len(shapes) :]
        fetches, stores = [], []
        if with_tokens:
            whole_chunk = pl.ds(start, width)
            sources = [ins[2].at[:, whole_chunk], ins[3].at[:, whole_chunk], ins[4].at[whole_chunk]]
            fetches = [
                pltpu.make_async_copy(source, buffers[i], buffers[3].at[i])
                for i, source in enumerate(sources)
            ]
            for i in (2, 0, 1):
                fetches[i].start()
        for i in range(3):
            acts[i, :half] = ins[0][i]
            acts[i, half:] = ins[1][i]
        if with_weights:
            xt_ref, c_ref = ins[n_token_args : n_token_args + 2]
            *staged, sem = buffers[-4:]
            for number, (at, size) in enumerate(tiles):
                here, there = pl.ds(at, size), pl.ds(start + at, size)
                for i in range(3):
                    if i < 2:
                        value = jnp.dot(
                            xt_ref[...], acts[i + 1, :, here], preferred_element_type=F32
                        )
                        source, target = staged[i].at[:, here], outs[i - 3].at[:, there]
                    else:
                        value = jnp.dot(
                            acts[0, :, here].T, c_ref[...], preferred_element_type=F32
                        )
                        source, target = staged[i].at[here], outs[i - 3].at[there]
                    source[...] = value.astype(BF16)
                    stores.append(pltpu.make_async_copy(source, target, sem.at[number, i]))
                    stores[-1].start()
        if with_tokens:
            total_ref = outs[0]
            fetches[2].wait()
            mixed = jnp.dot(acts[0], buffers[2][...], preferred_element_type=F32)
            total_ref[0] = mixed if total is None else total_ref[0] + mixed
            fetches[0].wait()
            fetches[1].wait()
            inputs = contract_last(acts[1], buffers[0][...]) + contract_last(
                acts[2], buffers[1][...]
            )
            total_ref[1] = inputs if total is None else total_ref[1] + inputs
        for store in stores:
            store.wait()

    out = order.call(
        kernel, (1,), specs, out_specs, shapes, aliases, KERNEL_VMEM, 1000,
        "backward_products", *args, scratch=scratch,
    )
    return (out[0] if with_tokens else total), (out[-3:] if with_weights else grads)


def in_vmem(array):
    return pltpu.with_memory_space_constraint(array, pltpu.VMEM)


def both_cores(pairs):
    return [(2 * a + core, 2 * b + core) for a, b in pairs for core in range(2)]


def shards(n_row, n_col, tokens, gate_weight, up_weight, down_weight, cotangent):
    chips = n_row // 2
    middle = chips // 2
    core = lax.axis_index("row") % 2
    chip = lax.axis_index("row") // 2
    siblings = [(r, r ^ 1) for r in range(n_row)]
    inward = [both_cores([(j, j + 1), (chips - 1 - j, chips - 2 - j)]) for j in range(middle - 1)]
    across = both_cores([(middle - 1, middle), (middle, middle - 1)])
    flags = [
        jnp.where((chip == j) | (chip == chips - 1 - j), 1, 0).astype(jnp.int32).reshape(1)
        for j in range(middle - 1)
    ]
    weights = [
        pltpu.with_memory_space_constraint(w, pltpu.HBM)
        for w in (gate_weight, up_weight, down_weight)
    ]

    order = Order()
    core_flag = core.astype(jnp.int32).reshape(1)

    def travel(block):
        return [block] + [
            lax.ppermute(block, "col", [(s, s ^ j) for s in range(n_col)]) for j in range(1, n_col)
        ]

    token_blocks, cotangent_blocks = travel(tokens), travel(cotangent)
    x = assemble(order, core_flag, token_blocks)

    chunks = chunks_of(gate_weight.shape[1])
    count = len(chunks)
    swapped, partial, arrived, acts, other = {}, {}, {}, {}, {}
    state = [None, None]

    def step_sums(k, partly=None):
        if 0 <= k < count:
            left = x if partly is None else None
            mine, theirs = forward(order, left, c, weights, *chunks[k], partly)
            swapped[k] = (mine, in_vmem(lax.ppermute(theirs, "row", siblings)))

    def step_chip(k):
        if 0 <= k < count:
            partial[k] = elementwise(order, add_kernel, "chip_sum", *swapped.pop(k))
            if inward:
                arrived[k] = in_vmem(lax.ppermute(partial[k], "row", inward[0]))

    def step_half(k):
        if 0 <= k < count:
            for hop in range(len(inward)):
                partial[k] = elementwise(order, add_kernel, "half_sum", partial[k], arrived[k])
                if hop + 1 < len(inward):
                    arrived[k] = in_vmem(lax.ppermute(partial[k], "row", inward[hop + 1]))
            arrived[k] = in_vmem(lax.ppermute(partial[k], "row", across))

    def step_act(k):
        if 0 <= k < count:
            acts[k] = elementwise(
                order, activation_kernel, "activations", partial.pop(k), arrived.pop(k)
            )
            if inward:
                back = [(t, s) for s, t in inward[-1]]
                arrived[k] = in_vmem(lax.ppermute(acts[k], "row", back))

    def step_choose(k):
        if 0 <= k < count:
            for hop in reversed(range(len(inward))):
                acts[k] = elementwise(
                    order, choose_kernel, "choose", acts[k], flags[hop], arrived[k]
                )
                if hop > 0:
                    back = [(t, s) for s, t in inward[hop - 1]]
                    arrived[k] = in_vmem(lax.ppermute(acts[k], "row", back))
            other[k] = in_vmem(lax.ppermute(acts[k], "row", siblings))

    def step_back(k, parts=("tokens", "weights")):
        if 0 <= k < count:
            state[0], state[1] = backward(
                order, acts[k], other[k], xt, c, weights, chunks[k][0], *state, parts
            )

    early = forward(order, x, None, weights, *chunks[0])
    c = assemble(order, core_flag, cotangent_blocks)
    step_sums(0, early)
    step_sums(1)
    step_chip(0)
    step_chip(1)
    summed = 2
    for k in range(count):
        fresh = range(summed, min(count, summed + (3 if k == 0 else 2)))
        summed = fresh.stop
        for j in fresh:
            step_sums(j)
        if k == 0:
            xt = transpose(order, x)
        step_half(k)
        step_act(k - 1)
        step_choose(k - 2)
        for j in fresh:
            step_chip(j)
        step_back(k - 3, ("tokens",) if k >= count - 2 else ("tokens", "weights"))
    step_act(count - 1)
    step_back(count - 5, ("weights",))
    step_choose(count - 2)
    step_back(count - 3)
    step_choose(count - 1)
    step_back(count - 2, ("tokens",))
    step_back(count - 1, ("tokens",))
    total = state[0]

    half = total.shape[1] // 2
    block = total.shape[1] // n_col
    total = total.astype(BF16)
    ordered = jnp.where(
        core == 0, total, jnp.concatenate([total[:, half:], total[:, :half]], axis=1)
    )
    out = ordered[:, :block].astype(F32)
    for j in range(1, n_col):
        piece = ordered[:, j * block : (j + 1) * block]
        out += lax.ppermute(piece, "col", [(s, s ^ j) for s in range(n_col)]).astype(F32)
    out = out.astype(BF16)
    for k in (count - 4, count - 2, count - 1):
        step_back(k, ("weights",))
    return out[0], out[1], *state[1]


def solution(mesh):
    in_specs = (P("col", "row"), P("row", "col"), P("row", "col"), P("col", "row"), P("col", "row"))
    out_specs = (
        P("col", "row"),
        P("col", "row"),
        P("row", "col"),
        P("row", "col"),
        P("col", "row"),
    )
    return jax.shard_map(
        functools.partial(shards, mesh.shape["row"], mesh.shape["col"]),
        mesh=mesh,
        in_specs=in_specs,
        out_specs=out_specs,
        check_vma=False,
    )
```

```python
import functools

import jax
import jax.numpy as jnp
from jax import lax
from jax.experimental import pallas as pl
from jax.experimental.pallas import tpu as pltpu
from jax.sharding import PartitionSpec as P

F32 = jnp.float32
BF16 = jnp.bfloat16
PROFILE = (3, 3, 3, 3, 3, 3, 3, 3, 2)
UNIT = 128
TILE = 256
PRODUCT_VMEM = 24 * 1024 * 1024
SUMS_VMEM = 12 * 1024 * 1024
SMALL_VMEM = 6 * 1024 * 1024
ANYWHERE = pl.BlockSpec(memory_space=pl.ANY)
RESIDENT = pl.BlockSpec(memory_space=pltpu.VMEM)


def chunks_of(hidden_units):
    unit = TILE if hidden_units % TILE == 0 else UNIT
    ends = [
        sum(PROFILE[: k + 1]) * (hidden_units // unit) // sum(PROFILE) for k in range(len(PROFILE))
    ]
    bounds = sorted({0, *ends})
    return [(s * unit, (e - s) * unit) for s, e in zip(bounds, bounds[1:])]


def tiles_of(width):
    return [(t, min(TILE, width - t)) for t in range(0, width, TILE)]


def contract_last(left, right):
    return lax.dot_general(left, right, (((1,), (1,)), ((), ())), preferred_element_type=F32)


def whole(shape):
    return pl.BlockSpec(shape, lambda i: (0,) * len(shape))


class Order:
    def __init__(self):
        self.last = None

    def call(self, kernel, grid, in_specs, out_specs, out_shape, aliases, vmem, cost, name, *args,
             scratch=()):
        extra = [] if self.last is None or any(self.last is a for a in args) else [self.last]
        extra = [pltpu.with_memory_space_constraint(e, pltpu.HBM) if e.ndim == 2 else e for e in extra]

        def body(*refs):
            kernel(*refs[: len(args)], *refs[len(args) + len(extra) :])

        out = pl.pallas_call(
            body,
            grid=grid,
            in_specs=list(in_specs) + [ANYWHERE] * len(extra),
            out_specs=out_specs,
            out_shape=out_shape,
            input_output_aliases=aliases,
            scratch_shapes=list(scratch),
            compiler_params=pltpu.CompilerParams(vmem_limit_bytes=vmem),
            cost_estimate=pl.CostEstimate(flops=cost, bytes_accessed=cost // 256, transcendentals=0),
            name=name,
        )(*args, *extra)
        self.last = out[0]
        return out


def split_store(values, mine_ref, theirs_ref):
    half = mine_ref.shape[1]
    for index, value in enumerate(values):
        mine_ref[index] = value[:half].astype(BF16)
        theirs_ref[index] = value[half:].astype(BF16)


def gate_up_sums(x_ref, gate_ref, up_ref):
    return [
        jnp.dot(x_ref[...], w_ref[...], preferred_element_type=F32) for w_ref in (gate_ref, up_ref)
    ]


def forward_kernel(x_ref, gate_ref, up_ref, c_ref, down_ref, mine_ref, theirs_ref):
    sums = gate_up_sums(x_ref, gate_ref, up_ref)
    split_store(sums + [contract_last(c_ref[...], down_ref[...])], mine_ref, theirs_ref)


def gate_up_kernel(x_ref, gate_ref, up_ref, mine_ref, theirs_ref):
    split_store(gate_up_sums(x_ref, gate_ref, up_ref), mine_ref, theirs_ref)


def back_kernel(c_ref, down_ref, mine_in_ref, theirs_in_ref, mine_ref, theirs_ref):
    split_store([contract_last(c_ref[...], down_ref[...])], mine_ref, theirs_ref)


def forward(order, x, c, weights, start, width, partly=None):
    tokens, depth = (c if x is None else x).shape
    tile = TILE if width % TILE == 0 and start % TILE == 0 else UNIT
    first = start // tile
    half = tokens // 2
    gate, up, down = weights
    part = pltpu.VMEM((3, half, width), BF16)
    column = pl.BlockSpec((depth, tile), lambda i: (0, first + i))
    row = pl.BlockSpec((tile, depth), lambda i: (first + i, 0))
    block = whole((tokens, depth))
    if c is None:
        kernel, specs, args = gate_up_kernel, [block, column, column], [x, gate, up]
        piece = pl.BlockSpec((2, half, tile), lambda i: (0, 0, i))
        aliases = {}
    elif x is None:
        kernel, specs, args = back_kernel, [block, row, ANYWHERE, ANYWHERE], [c, down, *partly]
        piece = pl.BlockSpec((1, half, tile), lambda i: (2, 0, i))
        aliases = {2: 0, 3: 1}
    else:
        kernel, specs = forward_kernel, [block, column, column, block, row]
        args = [x, gate, up, c, down]
        piece = pl.BlockSpec((3, half, tile), lambda i: (0, 0, i))
        aliases = {}
    return order.call(
        kernel, (width // tile,), specs, [piece, piece], [part, part], aliases, SUMS_VMEM, 1000,
        "forward_sums", *args,
    )


def elementwise(order, kernel, name, *args):
    piece = whole(args[0].shape)
    specs = [piece if a.ndim == 3 else pl.BlockSpec(memory_space=pltpu.SMEM) for a in args]
    shape = pltpu.VMEM(args[0].shape, BF16)
    return order.call(
        kernel, (1,), specs, [piece], [shape], {}, SMALL_VMEM, 1000, name, *args
    )[0]


def assemble_kernel(row_ref, *refs):
    blocks, out_ref = refs[:-1], refs[-1]
    count, rows = len(blocks), blocks[0].shape[0]
    for core in range(2):

        @pl.when(lax.rem(row_ref[0], 2) == core)
        def _():
            for index, block in enumerate(blocks):
                place = (index + core * (count // 2)) % count
                out_ref[pl.ds(place * rows, rows), :] = block[...]


def assemble(order, row, blocks):
    rows, depth = blocks[0].shape
    shape = (rows * len(blocks), depth)
    return order.call(
        assemble_kernel, (1,),
        [pl.BlockSpec(memory_space=pltpu.SMEM)] + [whole((rows, depth))] * len(blocks),
        [whole(shape)], [jax.ShapeDtypeStruct(shape, BF16)], {}, SMALL_VMEM, 1000,
        "assemble_tokens", row, *blocks,
    )[0]


def cut_kernel(row_ref, total_ref, *block_refs):
    count, rows = len(block_refs), block_refs[0].shape[1]
    for core in range(2):

        @pl.when(lax.rem(row_ref[0], 2) == core)
        def _():
            for index, block in enumerate(block_refs):
                place = (index + core * (count // 2)) % count
                block[...] = total_ref[:, pl.ds(place * rows, rows), :].astype(BF16)


def cut(order, row, total, count):
    _, tokens, depth = total.shape
    shape = (2, tokens // count, depth)
    return order.call(
        cut_kernel, (1,), [pl.BlockSpec(memory_space=pltpu.SMEM), RESIDENT], [whole(shape)] * count,
        [jax.ShapeDtypeStruct(shape, BF16)] * count, {}, SMALL_VMEM, 1000, "cut_totals", row, total,
    )


def transpose_kernel(x_ref, xt_ref):
    xt_ref[...] = x_ref[...].T


def transpose(order, x):
    shape = x.shape[::-1]
    return order.call(
        transpose_kernel, (1,), [whole(x.shape)], [whole(shape)],
        [jax.ShapeDtypeStruct(shape, BF16)], {}, SMALL_VMEM, 1000, "transpose_tokens", x,
    )[0]


def add_kernel(left_ref, right_ref, out_ref):
    out_ref[...] = (left_ref[...].astype(F32) + right_ref[...].astype(F32)).astype(BF16)


def choose_kernel(first, last, left_ref, row_ref, right_ref, out_ref):
    chip = lax.div(row_ref[0], 2)
    outer = (chip == first) | (chip == last)

    @pl.when(jnp.logical_not(outer))
    def _():
        out_ref[...] = left_ref[...]

    @pl.when(outer)
    def _():
        out_ref[...] = right_ref[...]


def activation_kernel(left_ref, right_ref, out_ref):
    gate_sum, up_sum, back_sum = (
        left_ref[i].astype(F32) + right_ref[i].astype(F32) for i in range(3)
    )
    sigma = jax.nn.sigmoid(gate_sum)
    silu = gate_sum * sigma
    out_ref[0] = (silu * up_sum).astype(BF16)
    out_ref[1] = (back_sum * up_sum * sigma * (1.0 + gate_sum * (1.0 - sigma))).astype(BF16)
    out_ref[2] = (back_sum * silu).astype(BF16)


def backward(order, mine, other, xt, c, weights, start, total, grads, parts):
    _, half, width = mine.shape
    tokens, depth = c.shape
    tiles = tiles_of(width)
    with_tokens, with_weights = "tokens" in parts, "weights" in parts
    piece = whole(mine.shape)
    specs, args, out_specs, shapes, aliases = [piece, piece], [mine, other], [], [], {}
    if with_tokens:
        specs += [ANYWHERE] * 3
        args += weights
        if total is not None:
            aliases[len(args)] = 0
            specs += [RESIDENT]
            args += [total]
        out_specs += [RESIDENT]
        shapes += [jax.ShapeDtypeStruct((2,) + c.shape, F32)]
    n_token_args = len(args)
    if with_weights:
        specs += [whole(xt.shape), whole(c.shape)]
        args += [xt, c]
        for index, grad in enumerate(grads or ()):
            aliases[len(args)] = len(out_specs) + index
            specs += [ANYWHERE]
            args += [grad]
        out_specs += [ANYWHERE] * 3
        shapes += [pltpu.HBM(w.shape, BF16) for w in weights]
    slab = [
        pltpu.VMEM((depth, width), BF16),
        pltpu.VMEM((depth, width), BF16),
        pltpu.VMEM((width, depth), BF16),
    ]
    scratch = [pltpu.VMEM((3, tokens, width), BF16)]
    scratch += (slab + [pltpu.SemaphoreType.DMA((3,))]) if with_tokens else []
    scratch += (slab + [pltpu.SemaphoreType.DMA((len(tiles), 3))]) if with_weights else []

    def kernel(*refs):
        ins = refs[: len(args)]
        outs = refs[len(args) : len(args) + len(shapes)]
        acts, *buffers = refs[len(args) + len(shapes) :]
        fetches, stores = [], []
        if with_tokens:
            whole_chunk = pl.ds(start, width)
            sources = [ins[2].at[:, whole_chunk], ins[3].at[:, whole_chunk], ins[4].at[whole_chunk]]
            fetches = [
                pltpu.make_async_copy(source, buffers[i], buffers[3].at[i])
                for i, source in enumerate(sources)
            ]
            for i in (2, 0, 1):
                fetches[i].start()
        for i in range(3):
            acts[i, :half] = ins[0][i]
            acts[i, half:] = ins[1][i]
        if with_weights:
            xt_ref, c_ref = ins[n_token_args : n_token_args + 2]
            *staged, sem = buffers[-4:]
            for number, (at, size) in enumerate(tiles):
                here, there = pl.ds(at, size), pl.ds(start + at, size)
                for i in range(3):
                    if i < 2:
                        value = jnp.dot(
                            xt_ref[...], acts[i + 1, :, here], preferred_element_type=F32
                        )
                        source, target = staged[i].at[:, here], outs[i - 3].at[:, there]
                    else:
                        value = jnp.dot(
                            acts[0, :, here].T, c_ref[...], preferred_element_type=F32
                        )
                        source, target = staged[i].at[here], outs[i - 3].at[there]
                    source[...] = value.astype(BF16)
                    stores.append(pltpu.make_async_copy(source, target, sem.at[number, i]))
                    stores[-1].start()
        if with_tokens:
            total_ref = outs[0]
            fetches[2].wait()
            mixed = jnp.dot(acts[0], buffers[2][...], preferred_element_type=F32)
            total_ref[0] = mixed if total is None else total_ref[0] + mixed
            fetches[0].wait()
            fetches[1].wait()
            inputs = contract_last(acts[1], buffers[0][...]) + contract_last(
                acts[2], buffers[1][...]
            )
            total_ref[1] = inputs if total is None else total_ref[1] + inputs
        for store in stores:
            store.wait()

    out = order.call(
        kernel, (1,), specs, out_specs, shapes, aliases, PRODUCT_VMEM, 1000,
        "backward_products", *args, scratch=scratch,
    )
    return (out[0] if with_tokens else total), (out[-3:] if with_weights else grads)


def in_vmem(array):
    return pltpu.with_memory_space_constraint(array, pltpu.VMEM)


def both_cores(pairs):
    return [(2 * a + core, 2 * b + core) for a, b in pairs for core in range(2)]


def shards(n_row, n_col, tokens, gate_weight, up_weight, down_weight, cotangent):
    chips = n_row // 2
    middle = chips // 2
    row = lax.axis_index("row").astype(jnp.int32).reshape(1)
    siblings = [(r, r ^ 1) for r in range(n_row)]
    inward = [both_cores([(j, j + 1), (chips - 1 - j, chips - 2 - j)]) for j in range(middle - 1)]
    across = both_cores([(middle - 1, middle), (middle, middle - 1)])
    weights = [
        pltpu.with_memory_space_constraint(w, pltpu.HBM)
        for w in (gate_weight, up_weight, down_weight)
    ]

    order = Order()

    def travel(block):
        return [block] + [
            lax.ppermute(block, "col", [(s, s ^ j) for s in range(n_col)]) for j in range(1, n_col)
        ]

    token_blocks, cotangent_blocks = travel(tokens), travel(cotangent)
    x = assemble(order, row, token_blocks)

    chunks = chunks_of(gate_weight.shape[1])
    count = len(chunks)
    swapped, partial, arrived, acts, other = {}, {}, {}, {}, {}
    state = [None, None]

    def step_sums(k, partly=None):
        if 0 <= k < count:
            left = x if partly is None else None
            mine, theirs = forward(order, left, c, weights, *chunks[k], partly)
            swapped[k] = (mine, in_vmem(lax.ppermute(theirs, "row", siblings)))

    def step_chip(k):
        if 0 <= k < count:
            partial[k] = elementwise(order, add_kernel, "chip_sum", *swapped.pop(k))
            if inward:
                arrived[k] = in_vmem(lax.ppermute(partial[k], "row", inward[0]))

    def step_half(k):
        if 0 <= k < count:
            for hop in range(len(inward)):
                partial[k] = elementwise(order, add_kernel, "half_sum", partial[k], arrived[k])
                if hop + 1 < len(inward):
                    arrived[k] = in_vmem(lax.ppermute(partial[k], "row", inward[hop + 1]))
            arrived[k] = in_vmem(lax.ppermute(partial[k], "row", across))

    def step_act(k):
        if 0 <= k < count:
            acts[k] = elementwise(
                order, activation_kernel, "activations", partial.pop(k), arrived.pop(k)
            )
            if inward:
                back = [(t, s) for s, t in inward[-1]]
                arrived[k] = in_vmem(lax.ppermute(acts[k], "row", back))

    def step_choose(k):
        if 0 <= k < count:
            for hop in reversed(range(len(inward))):
                acts[k] = elementwise(
                    order, functools.partial(choose_kernel, hop, chips - 1 - hop), "choose",
                    acts[k], row, arrived[k],
                )
                if hop > 0:
                    back = [(t, s) for s, t in inward[hop - 1]]
                    arrived[k] = in_vmem(lax.ppermute(acts[k], "row", back))
            other[k] = in_vmem(lax.ppermute(acts[k], "row", siblings))

    def step_back(k, parts=("tokens", "weights")):
        if 0 <= k < count:
            state[0], state[1] = backward(
                order, acts[k], other[k], xt, c, weights, chunks[k][0], *state, parts
            )

    early = forward(order, x, None, weights, *chunks[0])
    c = assemble(order, row, cotangent_blocks)
    step_sums(0, early)
    step_sums(1)
    step_chip(0)
    step_chip(1)
    summed = 2
    for k in range(count):
        fresh = range(summed, min(count, summed + (3 if k == 0 else 2)))
        summed = fresh.stop
        for j in fresh:
            step_sums(j)
        if k == 0:
            xt = transpose(order, x)
        step_half(k)
        step_act(k - 1)
        step_choose(k - 2)
        for j in fresh:
            step_chip(j)
        step_back(k - 3, ("tokens",) if k >= count - 2 else ("tokens", "weights"))
    step_act(count - 1)
    step_back(count - 5, ("weights",))
    step_choose(count - 2)
    step_back(count - 3)
    step_choose(count - 1)
    step_back(count - 2, ("tokens",))
    step_back(count - 1, ("tokens",))
    total = state[0]

    blocks = cut(order, row, total, n_col)
    out = blocks[0].astype(F32)
    for j in range(1, n_col):
        out += lax.ppermute(blocks[j], "col", [(s, s ^ j) for s in range(n_col)]).astype(F32)
    out = out.astype(BF16)
    for k in (count - 4, count - 2, count - 1):
        step_back(k, ("weights",))
    return out[0], out[1], *state[1]


def solution(mesh):
    in_specs = (P("col", "row"), P("row", "col"), P("row", "col"), P("col", "row"), P("col", "row"))
    out_specs = (
        P("col", "row"),
        P("col", "row"),
        P("row", "col"),
        P("row", "col"),
        P("col", "row"),
    )
    return jax.shard_map(
        functools.partial(shards, mesh.shape["row"], mesh.shape["col"]),
        mesh=mesh,
        in_specs=in_specs,
        out_specs=out_specs,
        check_vma=False,
    )
```

```python
import functools

import jax
import jax.numpy as jnp
from jax import lax
from jax.experimental import pallas as pl
from jax.experimental.pallas import tpu as pltpu
from jax.sharding import PartitionSpec as P

F32 = jnp.float32
BF16 = jnp.bfloat16
PROFILE = (3, 3, 3, 3, 3, 3, 3, 3, 2)
UNIT = 128
TILE = 256
PRODUCT_VMEM = 24 * 1024 * 1024
SUMS_VMEM = 12 * 1024 * 1024
SMALL_VMEM = 6 * 1024 * 1024
ANYWHERE = pl.BlockSpec(memory_space=pl.ANY)
RESIDENT = pl.BlockSpec(memory_space=pltpu.VMEM)


def chunks_of(hidden_units):
    unit = TILE if hidden_units % TILE == 0 else UNIT
    ends = [
        sum(PROFILE[: k + 1]) * (hidden_units // unit) // sum(PROFILE) for k in range(len(PROFILE))
    ]
    bounds = sorted({0, *ends})
    return [(s * unit, (e - s) * unit) for s, e in zip(bounds, bounds[1:])]


def tiles_of(width):
    return [(t, min(TILE, width - t)) for t in range(0, width, TILE)]


def contract_last(left, right):
    return lax.dot_general(left, right, (((1,), (1,)), ((), ())), preferred_element_type=F32)


def whole(shape):
    return pl.BlockSpec(shape, lambda i: (0,) * len(shape))


class Order:
    def __init__(self):
        self.last = None

    def call(self, kernel, grid, in_specs, out_specs, out_shape, aliases, vmem, cost, name, *args,
             scratch=()):
        extra = [] if self.last is None or any(self.last is a for a in args) else [self.last]
        extra = [pltpu.with_memory_space_constraint(e, pltpu.HBM) if e.ndim == 2 else e for e in extra]

        def body(*refs):
            kernel(*refs[: len(args)], *refs[len(args) + len(extra) :])

        out = pl.pallas_call(
            body,
            grid=grid,
            in_specs=list(in_specs) + [ANYWHERE] * len(extra),
            out_specs=out_specs,
            out_shape=out_shape,
            input_output_aliases=aliases,
            scratch_shapes=list(scratch),
            compiler_params=pltpu.CompilerParams(vmem_limit_bytes=vmem),
            cost_estimate=pl.CostEstimate(flops=cost, bytes_accessed=cost // 256, transcendentals=0),
            name=name,
        )(*args, *extra)
        self.last = out[0]
        return out


def forward(order, x, c, weights, start, width, partly=None):
    tokens, depth = (c if x is None else x).shape
    tile = TILE if width % TILE == 0 and start % TILE == 0 else UNIT
    tiles = width // tile
    half = tokens // 2
    wanted = ([0, 1] if x is not None else []) + ([2] if c is not None else [])
    sides = [a for a in (x, c) if a is not None]
    kept = list(partly or ())
    part = pltpu.VMEM((3, half, width), BF16)
    n_ins = len(sides) + len(wanted) + len(kept)

    def kernel(*refs):
        side_refs, weight_refs = refs[: len(sides)], refs[len(sides) : len(sides) + len(wanted)]
        mine_ref, theirs_ref, *buffers, sem = refs[n_ins:]

        def fetch(number, place):
            there = pl.ds(start + number * tile, tile)
            source = weight_refs[place]
            source = source.at[there] if wanted[place] == 2 else source.at[:, there]
            return pltpu.make_async_copy(source, buffers[place].at[number], sem.at[number, place])

        for number in range(tiles):
            for place in range(len(wanted)):
                fetch(number, place).start()

        @pl.loop(0, tiles)
        def _(number):
            here = pl.ds(pl.multiple_of(number * tile, tile), tile)
            for place, which in enumerate(wanted):
                fetch(number, place).wait()
                if which == 2:
                    value = contract_last(side_refs[-1][...], buffers[place][number])
                else:
                    value = jnp.dot(
                        side_refs[0][...], buffers[place][number], preferred_element_type=F32
                    )
                mine_ref[which, :, here] = value[:half].astype(BF16)
                theirs_ref[which, :, here] = value[half:].astype(BF16)

    spec = RESIDENT if kept else whole((3, half, width))
    return order.call(
        kernel, (1,),
        [whole(a.shape) for a in sides] + [ANYWHERE] * len(wanted) + [RESIDENT] * len(kept),
        [spec, spec], [part, part],
        {len(sides) + len(wanted) + i: i for i in range(len(kept))},
        SUMS_VMEM, 1000, "forward_sums",
        *sides, *[weights[w] for w in wanted], *kept,
        scratch=[
            pltpu.VMEM((tiles, tile, depth) if which == 2 else (tiles, depth, tile), BF16)
            for which in wanted
        ]
        + [pltpu.SemaphoreType.DMA((tiles, len(wanted)))],
    )


def elementwise(order, kernel, name, *args):
    piece = whole(args[0].shape)
    specs = [piece if a.ndim == 3 else pl.BlockSpec(memory_space=pltpu.SMEM) for a in args]
    shape = pltpu.VMEM(args[0].shape, BF16)
    return order.call(
        kernel, (1,), specs, [piece], [shape], {}, SMALL_VMEM, 1000, name, *args
    )[0]


def assemble_kernel(row_ref, *refs):
    blocks, out_ref = refs[:-1], refs[-1]
    count, rows = len(blocks), blocks[0].shape[0]
    for core in range(2):

        @pl.when(lax.rem(row_ref[0], 2) == core)
        def _():
            for index, block in enumerate(blocks):
                place = (index + core * (count // 2)) % count
                out_ref[pl.ds(place * rows, rows), :] = block[...]


def assemble(order, row, blocks):
    rows, depth = blocks[0].shape
    shape = (rows * len(blocks), depth)
    return order.call(
        assemble_kernel, (1,),
        [pl.BlockSpec(memory_space=pltpu.SMEM)] + [whole((rows, depth))] * len(blocks),
        [whole(shape)], [jax.ShapeDtypeStruct(shape, BF16)], {}, SMALL_VMEM, 1000,
        "assemble_tokens", row, *blocks,
    )[0]


def cut_kernel(row_ref, total_ref, *block_refs):
    count, rows = len(block_refs), block_refs[0].shape[1]
    for core in range(2):

        @pl.when(lax.rem(row_ref[0], 2) == core)
        def _():
            for index, block in enumerate(block_refs):
                place = (index + core * (count // 2)) % count
                block[...] = total_ref[:, pl.ds(place * rows, rows), :].astype(BF16)


def cut(order, row, total, count):
    _, tokens, depth = total.shape
    shape = (2, tokens // count, depth)
    return order.call(
        cut_kernel, (1,), [pl.BlockSpec(memory_space=pltpu.SMEM), RESIDENT], [whole(shape)] * count,
        [jax.ShapeDtypeStruct(shape, BF16)] * count, {}, SMALL_VMEM, 1000, "cut_totals", row, total,
    )


def transpose_kernel(x_ref, xt_ref):
    xt_ref[...] = x_ref[...].T


def transpose(order, x):
    shape = x.shape[::-1]
    return order.call(
        transpose_kernel, (1,), [whole(x.shape)], [whole(shape)],
        [jax.ShapeDtypeStruct(shape, BF16)], {}, SMALL_VMEM, 1000, "transpose_tokens", x,
    )[0]


def add_kernel(left_ref, right_ref, out_ref):
    out_ref[...] = (left_ref[...].astype(F32) + right_ref[...].astype(F32)).astype(BF16)


def choose_kernel(first, last, left_ref, row_ref, right_ref, out_ref):
    chip = lax.div(row_ref[0], 2)
    outer = (chip == first) | (chip == last)

    @pl.when(jnp.logical_not(outer))
    def _():
        out_ref[...] = left_ref[...]

    @pl.when(outer)
    def _():
        out_ref[...] = right_ref[...]


def activation_kernel(left_ref, right_ref, out_ref):
    gate_sum, up_sum, back_sum = (
        left_ref[i].astype(F32) + right_ref[i].astype(F32) for i in range(3)
    )
    sigma = jax.nn.sigmoid(gate_sum)
    silu = gate_sum * sigma
    out_ref[0] = (silu * up_sum).astype(BF16)
    out_ref[1] = (back_sum * up_sum * sigma * (1.0 + gate_sum * (1.0 - sigma))).astype(BF16)
    out_ref[2] = (back_sum * silu).astype(BF16)


def backward(order, mine, other, xt, c, weights, start, total, grads, parts):
    _, half, width = mine.shape
    tokens, depth = c.shape
    tiles = tiles_of(width)
    with_tokens, with_weights = "tokens" in parts, "weights" in parts
    piece = whole(mine.shape)
    specs, args, out_specs, shapes, aliases = [piece, piece], [mine, other], [], [], {}
    if with_tokens:
        specs += [ANYWHERE] * 3
        args += weights
        if total is not None:
            aliases[len(args)] = 0
            specs += [RESIDENT]
            args += [total]
        out_specs += [RESIDENT]
        shapes += [jax.ShapeDtypeStruct((2,) + c.shape, F32)]
    n_token_args = len(args)
    if with_weights:
        specs += [whole(xt.shape), whole(c.shape)]
        args += [xt, c]
        for index, grad in enumerate(grads or ()):
            aliases[len(args)] = len(out_specs) + index
            specs += [ANYWHERE]
            args += [grad]
        out_specs += [ANYWHERE] * 3
        shapes += [pltpu.HBM(w.shape, BF16) for w in weights]
    slab = [
        pltpu.VMEM((depth, width), BF16),
        pltpu.VMEM((depth, width), BF16),
        pltpu.VMEM((width, depth), BF16),
    ]
    scratch = [pltpu.VMEM((3, tokens, width), BF16)]
    scratch += (slab + [pltpu.SemaphoreType.DMA((3,))]) if with_tokens else []
    scratch += (slab + [pltpu.SemaphoreType.DMA((len(tiles), 3))]) if with_weights else []

    def kernel(*refs):
        ins = refs[: len(args)]
        outs = refs[len(args) : len(args) + len(shapes)]
        acts, *buffers = refs[len(args) + len(shapes) :]
        fetches, stores = [], []
        if with_tokens:
            whole_chunk = pl.ds(start, width)
            sources = [ins[2].at[:, whole_chunk], ins[3].at[:, whole_chunk], ins[4].at[whole_chunk]]
            fetches = [
                pltpu.make_async_copy(source, buffers[i], buffers[3].at[i])
                for i, source in enumerate(sources)
            ]
            for i in (2, 0, 1):
                fetches[i].start()
        for i in range(3):
            acts[i, :half] = ins[0][i]
            acts[i, half:] = ins[1][i]
        if with_weights:
            xt_ref, c_ref = ins[n_token_args : n_token_args + 2]
            *staged, sem = buffers[-4:]
            for number, (at, size) in enumerate(tiles):
                here, there = pl.ds(at, size), pl.ds(start + at, size)
                for i in range(3):
                    if i < 2:
                        value = jnp.dot(
                            xt_ref[...], acts[i + 1, :, here], preferred_element_type=F32
                        )
                        source, target = staged[i].at[:, here], outs[i - 3].at[:, there]
                    else:
                        value = jnp.dot(
                            acts[0, :, here].T, c_ref[...], preferred_element_type=F32
                        )
                        source, target = staged[i].at[here], outs[i - 3].at[there]
                    source[...] = value.astype(BF16)
                    stores.append(pltpu.make_async_copy(source, target, sem.at[number, i]))
                    stores[-1].start()
        if with_tokens:
            total_ref = outs[0]
            fetches[2].wait()
            mixed = jnp.dot(acts[0], buffers[2][...], preferred_element_type=F32)
            total_ref[0] = mixed if total is None else total_ref[0] + mixed
            fetches[0].wait()
            fetches[1].wait()
            inputs = contract_last(acts[1], buffers[0][...]) + contract_last(
                acts[2], buffers[1][...]
            )
            total_ref[1] = inputs if total is None else total_ref[1] + inputs
        for store in stores:
            store.wait()

    out = order.call(
        kernel, (1,), specs, out_specs, shapes, aliases, PRODUCT_VMEM, 1000,
        "backward_products", *args, scratch=scratch,
    )
    return (out[0] if with_tokens else total), (out[-3:] if with_weights else grads)


def in_vmem(array):
    return pltpu.with_memory_space_constraint(array, pltpu.VMEM)


def both_cores(pairs):
    return [(2 * a + core, 2 * b + core) for a, b in pairs for core in range(2)]


def shards(n_row, n_col, tokens, gate_weight, up_weight, down_weight, cotangent):
    chips = n_row // 2
    middle = chips // 2
    row = lax.axis_index("row").astype(jnp.int32).reshape(1)
    siblings = [(r, r ^ 1) for r in range(n_row)]
    inward = [both_cores([(j, j + 1), (chips - 1 - j, chips - 2 - j)]) for j in range(middle - 1)]
    across = both_cores([(middle - 1, middle), (middle, middle - 1)])
    weights = [
        pltpu.with_memory_space_constraint(w, pltpu.HBM)
        for w in (gate_weight, up_weight, down_weight)
    ]

    order = Order()

    def travel(block):
        return [block] + [
            lax.ppermute(block, "col", [(s, s ^ j) for s in range(n_col)]) for j in range(1, n_col)
        ]

    token_blocks, cotangent_blocks = travel(tokens), travel(cotangent)
    x = assemble(order, row, token_blocks)

    chunks = chunks_of(gate_weight.shape[1])
    count = len(chunks)
    swapped, partial, arrived, acts, other = {}, {}, {}, {}, {}
    state = [None, None]

    def step_sums(k, partly=None):
        if 0 <= k < count:
            left = x if partly is None else None
            mine, theirs = forward(order, left, c, weights, *chunks[k], partly)
            swapped[k] = (mine, in_vmem(lax.ppermute(theirs, "row", siblings)))

    def step_chip(k):
        if 0 <= k < count:
            partial[k] = elementwise(order, add_kernel, "chip_sum", *swapped.pop(k))
            if inward:
                arrived[k] = in_vmem(lax.ppermute(partial[k], "row", inward[0]))

    def step_half(k):
        if 0 <= k < count:
            for hop in range(len(inward)):
                partial[k] = elementwise(order, add_kernel, "half_sum", partial[k], arrived[k])
                if hop + 1 < len(inward):
                    arrived[k] = in_vmem(lax.ppermute(partial[k], "row", inward[hop + 1]))
            arrived[k] = in_vmem(lax.ppermute(partial[k], "row", across))

    def step_act(k):
        if 0 <= k < count:
            acts[k] = elementwise(
                order, activation_kernel, "activations", partial.pop(k), arrived.pop(k)
            )
            if inward:
                back = [(t, s) for s, t in inward[-1]]
                arrived[k] = in_vmem(lax.ppermute(acts[k], "row", back))

    def step_choose(k):
        if 0 <= k < count:
            for hop in reversed(range(len(inward))):
                acts[k] = elementwise(
                    order, functools.partial(choose_kernel, hop, chips - 1 - hop), "choose",
                    acts[k], row, arrived[k],
                )
                if hop > 0:
                    back = [(t, s) for s, t in inward[hop - 1]]
                    arrived[k] = in_vmem(lax.ppermute(acts[k], "row", back))
            other[k] = in_vmem(lax.ppermute(acts[k], "row", siblings))

    def step_back(k, parts=("tokens", "weights")):
        if 0 <= k < count:
            state[0], state[1] = backward(
                order, acts[k], other[k], xt, c, weights, chunks[k][0], *state, parts
            )

    early = forward(order, x, None, weights, *chunks[0])
    c = assemble(order, row, cotangent_blocks)
    step_sums(0, early)
    step_sums(1)
    step_chip(0)
    step_chip(1)
    summed = 2
    for k in range(count):
        fresh = range(summed, min(count, summed + (3 if k == 0 else 2)))
        summed = fresh.stop
        for j in fresh:
            step_sums(j)
        if k == 0:
            xt = transpose(order, x)
        step_half(k)
        step_act(k - 1)
        step_choose(k - 2)
        for j in fresh:
            step_chip(j)
        step_back(k - 3, ("tokens",) if k >= count - 2 else ("tokens", "weights"))
    step_act(count - 1)
    step_back(count - 5, ("weights",))
    step_choose(count - 2)
    step_back(count - 3)
    step_choose(count - 1)
    step_back(count - 2, ("tokens",))
    step_back(count - 1, ("tokens",))
    total = state[0]

    blocks = cut(order, row, total, n_col)
    out = blocks[0].astype(F32)
    for j in range(1, n_col):
        out += lax.ppermute(blocks[j], "col", [(s, s ^ j) for s in range(n_col)]).astype(F32)
    out = out.astype(BF16)
    for k in (count - 4, count - 2, count - 1):
        step_back(k, ("weights",))
    return out[0], out[1], *state[1]


def solution(mesh):
    in_specs = (P("col", "row"), P("row", "col"), P("row", "col"), P("col", "row"), P("col", "row"))
    out_specs = (
        P("col", "row"),
        P("col", "row"),
        P("row", "col"),
        P("row", "col"),
        P("col", "row"),
    )
    return jax.shard_map(
        functools.partial(shards, mesh.shape["row"], mesh.shape["col"]),
        mesh=mesh,
        in_specs=in_specs,
        out_specs=out_specs,
        check_vma=False,
    )
```

```python
import functools

import jax
import jax.numpy as jnp
from jax import lax
from jax.experimental import pallas as pl
from jax.experimental.pallas import tpu as pltpu
from jax.sharding import PartitionSpec as P

F32 = jnp.float32
BF16 = jnp.bfloat16
PROFILE = (3, 3, 3, 3, 3, 3, 3, 3, 2)
UNIT = 128
TILE = 256
SUM_TILES = (384, 256, 128)
PRODUCT_VMEM = 24 * 1024 * 1024
SUMS_VMEM = 16 * 1024 * 1024
SMALL_VMEM = 6 * 1024 * 1024
ANYWHERE = pl.BlockSpec(memory_space=pl.ANY)
RESIDENT = pl.BlockSpec(memory_space=pltpu.VMEM)


def chunks_of(hidden_units):
    unit = TILE if hidden_units % TILE == 0 else UNIT
    ends = [
        sum(PROFILE[: k + 1]) * (hidden_units // unit) // sum(PROFILE) for k in range(len(PROFILE))
    ]
    bounds = sorted({0, *ends})
    return [(s * unit, (e - s) * unit) for s, e in zip(bounds, bounds[1:])]


def tiles_of(width):
    return [(t, min(TILE, width - t)) for t in range(0, width, TILE)]


def contract_last(left, right):
    return lax.dot_general(left, right, (((1,), (1,)), ((), ())), preferred_element_type=F32)


def whole(shape):
    return pl.BlockSpec(shape, lambda i: (0,) * len(shape))


class Order:
    def __init__(self):
        self.last = None

    def call(self, kernel, grid, in_specs, out_specs, out_shape, aliases, vmem, cost, name, *args,
             scratch=()):
        extra = [] if self.last is None or any(self.last is a for a in args) else [self.last]
        extra = [pltpu.with_memory_space_constraint(e, pltpu.HBM) if e.ndim == 2 else e for e in extra]

        def body(*refs):
            kernel(*refs[: len(args)], *refs[len(args) + len(extra) :])

        out = pl.pallas_call(
            body,
            grid=grid,
            in_specs=list(in_specs) + [ANYWHERE] * len(extra),
            out_specs=out_specs,
            out_shape=out_shape,
            input_output_aliases=aliases,
            scratch_shapes=list(scratch),
            compiler_params=pltpu.CompilerParams(vmem_limit_bytes=vmem),
            cost_estimate=pl.CostEstimate(flops=cost, bytes_accessed=cost // 256, transcendentals=0),
            name=name,
        )(*args, *extra)
        self.last = out[0]
        return out


def split_store(values, mine_ref, theirs_ref):
    half = mine_ref.shape[1]
    for index, value in enumerate(values):
        mine_ref[index] = value[:half].astype(BF16)
        theirs_ref[index] = value[half:].astype(BF16)


def gate_up_sums(x_ref, gate_ref, up_ref):
    return [
        jnp.dot(x_ref[...], w_ref[...], preferred_element_type=F32) for w_ref in (gate_ref, up_ref)
    ]


def forward_kernel(x_ref, gate_ref, up_ref, c_ref, down_ref, mine_ref, theirs_ref):
    sums = gate_up_sums(x_ref, gate_ref, up_ref)
    split_store(sums + [contract_last(c_ref[...], down_ref[...])], mine_ref, theirs_ref)


def gate_up_kernel(x_ref, gate_ref, up_ref, mine_ref, theirs_ref):
    split_store(gate_up_sums(x_ref, gate_ref, up_ref), mine_ref, theirs_ref)


def back_kernel(c_ref, down_ref, mine_in_ref, theirs_in_ref, mine_ref, theirs_ref):
    split_store([contract_last(c_ref[...], down_ref[...])], mine_ref, theirs_ref)


def forward(order, x, c, weights, start, width, partly=None):
    tokens, depth = (c if x is None else x).shape
    tile = next(t for t in SUM_TILES if width % t == 0 and start % t == 0)
    first = start // tile
    half = tokens // 2
    gate, up, down = weights
    part = pltpu.VMEM((3, half, width), BF16)
    column = pl.BlockSpec((depth, tile), lambda i: (0, first + i))
    row = pl.BlockSpec((tile, depth), lambda i: (first + i, 0))
    block = whole((tokens, depth))
    if c is None:
        kernel, specs, args = gate_up_kernel, [block, column, column], [x, gate, up]
        piece = pl.BlockSpec((2, half, tile), lambda i: (0, 0, i))
        aliases = {}
    elif x is None:
        kernel, specs, args = back_kernel, [block, row, ANYWHERE, ANYWHERE], [c, down, *partly]
        piece = pl.BlockSpec((1, half, tile), lambda i: (2, 0, i))
        aliases = {2: 0, 3: 1}
    else:
        kernel, specs = forward_kernel, [block, column, column, block, row]
        args = [x, gate, up, c, down]
        piece = pl.BlockSpec((3, half, tile), lambda i: (0, 0, i))
        aliases = {}
    return order.call(
        kernel, (width // tile,), specs, [piece, piece], [part, part], aliases, SUMS_VMEM, 1000,
        "forward_sums", *args,
    )


def elementwise(order, kernel, name, *args):
    piece = whole(args[0].shape)
    specs = [piece if a.ndim == 3 else pl.BlockSpec(memory_space=pltpu.SMEM) for a in args]
    shape = pltpu.VMEM(args[0].shape, BF16)
    return order.call(
        kernel, (1,), specs, [piece], [shape], {}, SMALL_VMEM, 1000, name, *args
    )[0]


def assemble_kernel(row_ref, *refs):
    blocks, out_ref = refs[:-1], refs[-1]
    count, rows = len(blocks), blocks[0].shape[0]
    for core in range(2):

        @pl.when(lax.rem(row_ref[0], 2) == core)
        def _():
            for index, block in enumerate(blocks):
                place = (index + core * (count // 2)) % count
                out_ref[pl.ds(place * rows, rows), :] = block[...]


def assemble(order, row, blocks):
    rows, depth = blocks[0].shape
    shape = (rows * len(blocks), depth)
    return order.call(
        assemble_kernel, (1,),
        [pl.BlockSpec(memory_space=pltpu.SMEM)] + [whole((rows, depth))] * len(blocks),
        [whole(shape)], [jax.ShapeDtypeStruct(shape, BF16)], {}, SMALL_VMEM, 1000,
        "assemble_tokens", row, *blocks,
    )[0]


def cut_kernel(row_ref, total_ref, *block_refs):
    count, rows = len(block_refs), block_refs[0].shape[1]
    for core in range(2):

        @pl.when(lax.rem(row_ref[0], 2) == core)
        def _():
            for index, block in enumerate(block_refs):
                place = (index + core * (count // 2)) % count
                block[...] = total_ref[:, pl.ds(place * rows, rows), :].astype(BF16)


def cut(order, row, total, count):
    _, tokens, depth = total.shape
    shape = (2, tokens // count, depth)
    return order.call(
        cut_kernel, (1,), [pl.BlockSpec(memory_space=pltpu.SMEM), RESIDENT], [whole(shape)] * count,
        [jax.ShapeDtypeStruct(shape, BF16)] * count, {}, SMALL_VMEM, 1000, "cut_totals", row, total,
    )


def transpose_kernel(x_ref, xt_ref):
    xt_ref[...] = x_ref[...].T


def transpose(order, x):
    shape = x.shape[::-1]
    return order.call(
        transpose_kernel, (1,), [whole(x.shape)], [whole(shape)],
        [jax.ShapeDtypeStruct(shape, BF16)], {}, SMALL_VMEM, 1000, "transpose_tokens", x,
    )[0]


def add_kernel(left_ref, right_ref, out_ref):
    out_ref[...] = (left_ref[...].astype(F32) + right_ref[...].astype(F32)).astype(BF16)


def choose_kernel(first, last, left_ref, row_ref, right_ref, out_ref):
    chip = lax.div(row_ref[0], 2)
    outer = (chip == first) | (chip == last)

    @pl.when(jnp.logical_not(outer))
    def _():
        out_ref[...] = left_ref[...]

    @pl.when(outer)
    def _():
        out_ref[...] = right_ref[...]


def activation_kernel(left_ref, right_ref, out_ref):
    gate_sum, up_sum, back_sum = (
        left_ref[i].astype(F32) + right_ref[i].astype(F32) for i in range(3)
    )
    sigma = jax.nn.sigmoid(gate_sum)
    silu = gate_sum * sigma
    out_ref[0] = (silu * up_sum).astype(BF16)
    out_ref[1] = (back_sum * up_sum * sigma * (1.0 + gate_sum * (1.0 - sigma))).astype(BF16)
    out_ref[2] = (back_sum * silu).astype(BF16)


def backward(order, mine, other, xt, c, weights, start, total, grads, parts):
    _, half, width = mine.shape
    tokens, depth = c.shape
    tiles = tiles_of(width)
    with_tokens, with_weights = "tokens" in parts, "weights" in parts
    piece = whole(mine.shape)
    specs, args, out_specs, shapes, aliases = [piece, piece], [mine, other], [], [], {}
    if with_tokens:
        specs += [ANYWHERE] * 3
        args += weights
        if total is not None:
            aliases[len(args)] = 0
            specs += [RESIDENT]
            args += [total]
        out_specs += [RESIDENT]
        shapes += [jax.ShapeDtypeStruct((2,) + c.shape, F32)]
    n_token_args = len(args)
    if with_weights:
        specs += [whole(xt.shape), whole(c.shape)]
        args += [xt, c]
        for index, grad in enumerate(grads or ()):
            aliases[len(args)] = len(out_specs) + index
            specs += [ANYWHERE]
            args += [grad]
        out_specs += [ANYWHERE] * 3
        shapes += [pltpu.HBM(w.shape, BF16) for w in weights]
    slab = [
        pltpu.VMEM((depth, width), BF16),
        pltpu.VMEM((depth, width), BF16),
        pltpu.VMEM((width, depth), BF16),
    ]
    scratch = [pltpu.VMEM((3, tokens, width), BF16)]
    scratch += (slab + [pltpu.SemaphoreType.DMA((3,))]) if with_tokens else []
    scratch += (slab + [pltpu.SemaphoreType.DMA((len(tiles), 3))]) if with_weights else []

    def kernel(*refs):
        ins = refs[: len(args)]
        outs = refs[len(args) : len(args) + len(shapes)]
        acts, *buffers = refs[len(args) + len(shapes) :]
        fetches, stores = [], []
        if with_tokens:
            whole_chunk = pl.ds(start, width)
            sources = [ins[2].at[:, whole_chunk], ins[3].at[:, whole_chunk], ins[4].at[whole_chunk]]
            fetches = [
                pltpu.make_async_copy(source, buffers[i], buffers[3].at[i])
                for i, source in enumerate(sources)
            ]
            for i in (2, 0, 1):
                fetches[i].start()
        for i in range(3):
            acts[i, :half] = ins[0][i]
            acts[i, half:] = ins[1][i]
        if with_weights:
            xt_ref, c_ref = ins[n_token_args : n_token_args + 2]
            *staged, sem = buffers[-4:]
            for number, (at, size) in enumerate(tiles):
                here, there = pl.ds(at, size), pl.ds(start + at, size)
                for i in range(3):
                    if i < 2:
                        value = jnp.dot(
                            xt_ref[...], acts[i + 1, :, here], preferred_element_type=F32
                        )
                        source, target = staged[i].at[:, here], outs[i - 3].at[:, there]
                    else:
                        value = jnp.dot(
                            acts[0, :, here].T, c_ref[...], preferred_element_type=F32
                        )
                        source, target = staged[i].at[here], outs[i - 3].at[there]
                    source[...] = value.astype(BF16)
                    stores.append(pltpu.make_async_copy(source, target, sem.at[number, i]))
                    stores[-1].start()
        if with_tokens:
            total_ref = outs[0]
            fetches[2].wait()
            mixed = jnp.dot(acts[0], buffers[2][...], preferred_element_type=F32)
            total_ref[0] = mixed if total is None else total_ref[0] + mixed
            fetches[0].wait()
            fetches[1].wait()
            inputs = contract_last(acts[1], buffers[0][...]) + contract_last(
                acts[2], buffers[1][...]
            )
            total_ref[1] = inputs if total is None else total_ref[1] + inputs
        for store in stores:
            store.wait()

    out = order.call(
        kernel, (1,), specs, out_specs, shapes, aliases, PRODUCT_VMEM, 1000,
        "backward_products", *args, scratch=scratch,
    )
    return (out[0] if with_tokens else total), (out[-3:] if with_weights else grads)


def in_vmem(array):
    return pltpu.with_memory_space_constraint(array, pltpu.VMEM)


def both_cores(pairs):
    return [(2 * a + core, 2 * b + core) for a, b in pairs for core in range(2)]


def shards(n_row, n_col, tokens, gate_weight, up_weight, down_weight, cotangent):
    chips = n_row // 2
    middle = chips // 2
    row = lax.axis_index("row").astype(jnp.int32).reshape(1)
    siblings = [(r, r ^ 1) for r in range(n_row)]
    inward = [both_cores([(j, j + 1), (chips - 1 - j, chips - 2 - j)]) for j in range(middle - 1)]
    across = both_cores([(middle - 1, middle), (middle, middle - 1)])
    weights = [
        pltpu.with_memory_space_constraint(w, pltpu.HBM)
        for w in (gate_weight, up_weight, down_weight)
    ]

    order = Order()

    def travel(block):
        return [block] + [
            lax.ppermute(block, "col", [(s, s ^ j) for s in range(n_col)]) for j in range(1, n_col)
        ]

    token_blocks, cotangent_blocks = travel(tokens), travel(cotangent)
    x = assemble(order, row, token_blocks)

    chunks = chunks_of(gate_weight.shape[1])
    count = len(chunks)
    swapped, partial, arrived, acts, other = {}, {}, {}, {}, {}
    state = [None, None]

    def step_sums(k, partly=None):
        if 0 <= k < count:
            left = x if partly is None else None
            mine, theirs = forward(order, left, c, weights, *chunks[k], partly)
            swapped[k] = (mine, in_vmem(lax.ppermute(theirs, "row", siblings)))

    def step_chip(k):
        if 0 <= k < count:
            partial[k] = elementwise(order, add_kernel, "chip_sum", *swapped.pop(k))
            if inward:
                arrived[k] = in_vmem(lax.ppermute(partial[k], "row", inward[0]))

    def step_half(k):
        if 0 <= k < count:
            for hop in range(len(inward)):
                partial[k] = elementwise(order, add_kernel, "half_sum", partial[k], arrived[k])
                if hop + 1 < len(inward):
                    arrived[k] = in_vmem(lax.ppermute(partial[k], "row", inward[hop + 1]))
            arrived[k] = in_vmem(lax.ppermute(partial[k], "row", across))

    def step_act(k):
        if 0 <= k < count:
            acts[k] = elementwise(
                order, activation_kernel, "activations", partial.pop(k), arrived.pop(k)
            )
            if inward:
                back = [(t, s) for s, t in inward[-1]]
                arrived[k] = in_vmem(lax.ppermute(acts[k], "row", back))

    def step_choose(k):
        if 0 <= k < count:
            for hop in reversed(range(len(inward))):
                acts[k] = elementwise(
                    order, functools.partial(choose_kernel, hop, chips - 1 - hop), "choose",
                    acts[k], row, arrived[k],
                )
                if hop > 0:
                    back = [(t, s) for s, t in inward[hop - 1]]
                    arrived[k] = in_vmem(lax.ppermute(acts[k], "row", back))
            other[k] = in_vmem(lax.ppermute(acts[k], "row", siblings))

    def step_back(k, parts=("tokens", "weights")):
        if 0 <= k < count:
            state[0], state[1] = backward(
                order, acts[k], other[k], xt, c, weights, chunks[k][0], *state, parts
            )

    early = forward(order, x, None, weights, *chunks[0])
    c = assemble(order, row, cotangent_blocks)
    step_sums(0, early)
    step_sums(1)
    step_chip(0)
    step_chip(1)
    summed = 2
    for k in range(count):
        fresh = range(summed, min(count, summed + (3 if k == 0 else 2)))
        summed = fresh.stop
        for j in fresh:
            step_sums(j)
        if k == 0:
            xt = transpose(order, x)
        step_half(k)
        step_act(k - 1)
        step_choose(k - 2)
        for j in fresh:
            step_chip(j)
        step_back(k - 3, ("tokens",) if k >= count - 2 else ("tokens", "weights"))
    step_act(count - 1)
    step_back(count - 5, ("weights",))
    step_choose(count - 2)
    step_back(count - 3)
    step_choose(count - 1)
    step_back(count - 2, ("tokens",))
    step_back(count - 1, ("tokens",))
    total = state[0]

    blocks = cut(order, row, total, n_col)
    out = blocks[0].astype(F32)
    for j in reversed(range(1, n_col)):
        out += lax.ppermute(blocks[j], "col", [(s, s ^ j) for s in range(n_col)]).astype(F32)
    out = out.astype(BF16)
    for k in (count - 4, count - 2, count - 1):
        step_back(k, ("weights",))
    return out[0], out[1], *state[1]


def solution(mesh):
    in_specs = (P("col", "row"), P("row", "col"), P("row", "col"), P("col", "row"), P("col", "row"))
    out_specs = (
        P("col", "row"),
        P("col", "row"),
        P("row", "col"),
        P("row", "col"),
        P("col", "row"),
    )
    return jax.shard_map(
        functools.partial(shards, mesh.shape["row"], mesh.shape["col"]),
        mesh=mesh,
        in_specs=in_specs,
        out_specs=out_specs,
        check_vma=False,
    )
```
